512 devices in a mesh: tm: 128 (over y, x, z_lo), head: 4 (over z_hi, core).
Axes of the slice: x: 4, y: 4, z: 16 (z_hi: 2, z_lo: 8; z = z_hi * 8 + z_lo), core: 2. Of those that a mesh axis runs over, the one named last changes fastest.
Arguments:
- latent: bfloat16 [128, 256, 1920], P('tm', None, 'head'), may hold values from -6 to 6
- start_frame: int32 [128], P('tm'), may hold values from 0 to 1
- norm_gains: float32 [2, 1920], replicated, may hold values from 0.1 to 1.9
- qkv_weight: bfloat16 [2, 1920, 3, 1024], P(None, 'tm', None, 'head')
- out_weight: bfloat16 [2, 1024, 1920], P(None, 'head', 'tm'), may hold values from -0.75 to 0.75
Outputs:
- refined: bfloat16 [128, 256, 1920], P('head', 'tm')
The draws below stay inside these ranges and needn't reach their ends.
All inputs are finite; a program needn't handle non-finite values.
Results may differ from the reference program's by a relative error of at most 0.035.
Values may be sent and summed in bfloat16 or wider, within the bound.
A program may use at most 64 MiB of HBM per device.

```python
import jax
import jax.numpy as jnp
from jax import lax

D = 1920
HEAD_DIM = 64
HEADS = 16
LAYERS = 2
CLIP_STRETCHES = 8
SPAN = 128
STRETCH_FRAMES = 2
FRAMES = 256
N_TM = 128
N_HEAD = 4


def draw_qkv_weight(key, part):
    key = jax.random.fold_in(key, 7)
    base = jax.random.normal(key, (LAYERS, D, 3, HEADS * HEAD_DIM), jnp.float32) * D ** (-0.5)
    return base.astype(jnp.bfloat16)


def set_ends(drawn, stream_key, least, largest):
    longest = drawn.shape.index(max(drawn.shape))
    spots = []
    for shift in (0, 1):
        where = [jax.random.randint(jax.random.fold_in(stream_key, axis), (), 0, length) for axis, length in enumerate(drawn.shape)]
        where[longest] = (where[longest] + shift) % drawn.shape[longest]
        spots.append(tuple(where))
    return drawn.at[spots[0]].set(least).at[spots[1]].set(largest)


def block_scale(stream_key, extent, cuts, smallest, top_value):
    level = 1.0
    for axis_at, shards_of in cuts:
        steps = jax.random.uniform(jax.random.fold_in(jax.random.fold_in(stream_key, 6), axis_at), (shards_of,), jnp.float32, smallest / len(cuts), top_value / len(cuts))
        level = level * jnp.repeat(jnp.exp(steps), extent[axis_at] // shards_of).reshape((-1,) + (1,) * (len(extent) - 1 - axis_at))
    return level


def noise(stream_key, shape, spread, most, cuts=(), kind=jnp.bfloat16):
    entries = spread * jax.random.normal(stream_key, shape, jnp.float32)
    if cuts:
        entries = entries * block_scale(stream_key, shape, cuts, -0.22, 0.18)
    return jnp.clip(entries, -most, most).astype(kind)


def setup_inputs(seed: int = 0) -> dict:
    key_of = jax.random.split(jax.random.key(seed), 6)
    return {
        "latent": noise(key_of[0], (SPAN, FRAMES, D), 1.0, 6.0, ((0, 128), (2, 4))),
        "start_frame": set_ends(jax.random.randint(key_of[1], (N_TM,), 0, STRETCH_FRAMES), jax.random.fold_in(key_of[1], 1), 0, STRETCH_FRAMES - 1).astype(jnp.int32),
        "norm_gains": jnp.clip(1.0 + 0.18 * jax.random.normal(key_of[2], (LAYERS, D), jnp.float32), 0.1, 1.9),
        "qkv_weight": draw_qkv_weight(jax.random.fold_in(key_of[5], 71), 0),
        "out_weight": noise(key_of[4], (LAYERS, HEADS * HEAD_DIM, D), HEAD_DIM ** -0.5, 0.75, ((1, 4), (2, 128))),
    }


EPSILON = 1e-06

def attend(queries, key_rows, value_rows, prev_keys, prev_values, visible):
    row_count = queries.shape[0]
    shaped = (row_count, HEADS, HEAD_DIM)
    factor = HEAD_DIM ** (-0.5)
    query_f = queries.astype(jnp.float32).reshape(shaped)
    own_scores = jnp.einsum('qhd,khd->hqk', query_f, key_rows.astype(jnp.float32).reshape(shaped)) * factor
    past_scores = jnp.einsum('qhd,khd->hqk', query_f, prev_keys.astype(jnp.float32).reshape(shaped)) * factor
    past_scores = jnp.where(visible[None, None, :], past_scores, -jnp.inf)
    scores = jnp.concatenate([own_scores, past_scores], axis=2)
    highest = lax.optimization_barrier(jnp.max(scores, axis=2, keepdims=True))
    exponent = jnp.exp(scores - highest)
    weights = (exponent / lax.optimization_barrier(jnp.sum(exponent, axis=2, keepdims=True))).astype(jnp.bfloat16)
    both_values = jnp.concatenate([value_rows, prev_values], axis=0).reshape(2 * row_count, HEADS, HEAD_DIM)
    blended = jnp.einsum('hqk,khd->qhd', weights.astype(jnp.float32), both_values.astype(jnp.float32))
    return blended.astype(jnp.bfloat16).reshape(row_count, HEADS * HEAD_DIM)

def reference(latent, start_frame, norm_gains, qkv_weight, out_weight):
    resident = latent.astype(jnp.float32)
    width = HEADS * HEAD_DIM
    group_width = width // N_HEAD
    row_count = SPAN * STRETCH_FRAMES
    frame_of = (jnp.arange(row_count) % STRETCH_FRAMES).astype(jnp.int32)
    stretch_ids = jnp.arange(N_TM).astype(jnp.int32)
    for layer_num in range(LAYERS):
        mean_square = lax.optimization_barrier(jnp.mean(resident * resident, axis=-1, keepdims=True))
        normed = (resident * lax.rsqrt(mean_square + EPSILON) * norm_gains[layer_num]).astype(jnp.bfloat16)
        stretches = normed.reshape(SPAN, N_TM, STRETCH_FRAMES, D).transpose(1, 0, 2, 3).reshape(N_TM, row_count, D)
        weight_mat = qkv_weight[layer_num].reshape(D, 3 * width)
        projected = lax.map(lambda rows_in: jnp.dot(rows_in, weight_mat, preferred_element_type=jnp.float32).astype(jnp.bfloat16), stretches)
        projected = projected.reshape(N_TM, row_count, 3, width)
        queries = projected[:, :, 0]
        key_rows = projected[:, :, 1]
        value_rows = projected[:, :, 2]
        prev_keys = jnp.concatenate([jnp.zeros_like(key_rows[:1]), key_rows[:-1]], axis=0)
        prev_values = jnp.concatenate([jnp.zeros_like(value_rows[:1]), value_rows[:-1]], axis=0)
        out_layer = out_weight[layer_num]

        def one_stretch(packed):
            query_c, key_c, value_c, pkey_c, pvalue_c, boundary, stretch_num = packed
            visible = (frame_of >= boundary) & (stretch_num % CLIP_STRETCHES > 0)
            blended = attend(query_c, key_c, value_c, pkey_c, pvalue_c, visible)
            running = jnp.zeros((row_count, D), jnp.float32)
            for group_num in range(N_HEAD):
                lower = group_num * group_width
                part = jnp.dot(blended[:, lower:lower + group_width], out_layer[lower:lower + group_width], preferred_element_type=jnp.float32)
                running = running + lax.optimization_barrier(part.astype(jnp.bfloat16)).astype(jnp.float32)
            return running
        summed = lax.map(one_stretch, (queries, key_rows, value_rows, prev_keys, prev_values, start_frame, stretch_ids))
        summed = summed.reshape(N_TM, SPAN, STRETCH_FRAMES, D).transpose(1, 0, 2, 3).reshape(SPAN, FRAMES, D)
        resident = resident + summed
    return resident.astype(jnp.bfloat16)
```

```python
import jax
import jax.numpy as jnp
from jax import lax
from jax.experimental import pallas as pl
from jax.experimental.pallas import tpu as pltpu
from jax.sharding import PartitionSpec as P

NX, NY, NZ, ZLO = 4, 4, 16, 8
LAYERS = 2
D = 1920
DP = 2048
QP = 512
EPSILON = 1e-06
F32, BF16 = jnp.float32, jnp.bfloat16
MESH = pl.DeviceIdType.MESH


def dot(a, b):
    return jnp.dot(a, b, preferred_element_type=F32)


def dot_t(a, b):
    return lax.dot_general(a, b, (((1,), (1,)), ((), ())), preferred_element_type=F32)


def iota(shape, dim):
    return lax.broadcasted_iota(jnp.int32, shape, dim)


def onehot(mask):
    return jnp.where(mask, 1.0, 0.0).astype(BF16)


def kernel(
    lat_ref, pad_ref, gain_ref, wloc_ref, out_ref,
    latp, r1, y1, xq, wz, wf, wos, resid, xn, qkv, pkv, blb, bls, gs, rsb, fo,
    az_s, az_r, ay_s, ay_r, wz_s, wz_r, wx_s, wx_r, wy_s, wy_r, wg_s, wg_r,
    wo_s, wo_r, ag_s, ag_r, kv_s, kv_r, bl_s, bl_r, rs_s, rs_r, fi_s, fi_r,
):
    tm, hd = lax.axis_index("tm"), lax.axis_index("head")
    y, x, zl = tm // 32, (tm // 8) % 4, tm % 8
    zh, c = hd // 2, hd % 2
    z = zh * 8 + zl

    def dev(xx, yy, zz, cc):
        return (yy * 32 + xx * 8 + zz % 8, (zz // 8) * 2 + cc)

    sends = []

    def send(src, dst, s_sem, r_sem, to):
        copy = pltpu.make_async_remote_copy(
            src_ref=src, dst_ref=dst, send_sem=s_sem, recv_sem=r_sem,
            device_id=to, device_id_type=MESH,
        )
        copy.start()
        sends.append(copy)

    def arrive(dst, sem):
        pltpu.make_async_copy(dst, dst, sem).wait()

    clip_x = z // 4
    pair = z % 4
    xu, xd, xo = (x + 1) % 4, (x + 3) % 4, (x + 2) % 4
    yu, yd, yo = (y + 1) % 4, (y + 3) % 4, (y + 2) % 4
    zu, zd = (z + 1) % 16, (z + 15) % 16

    barrier = pltpu.get_barrier_semaphore()

    def greet(to):
        pl.semaphore_signal(barrier, inc=1, device_id=to, device_id_type=MESH)

    for o in range(1, 16):
        greet(dev(x, y, (z + o) % 16, c))
    for o in range(4):
        for j in range(2):
            if o or j:
                greet(dev((x + o) % 4, y, z, (c + j) % 2))
    for o in range(1, 4):
        for j in range(2):
            greet(dev(x, (y + o) % 4, z, (c + j) % 2))
    for o in range(4):
        greet(dev((x + o) % 4, y, x * 4 + zl // 2, zl % 2))

    row, col = iota((256, 256), 0), iota((256, 256), 1)
    rows_by_z = onehot(col == ((row >> 2) & 3) * 64 + (row >> 4) * 4 + (row & 3))
    chan, pch = iota((480, QP), 0), iota((480, QP), 1)
    spread = onehot((chan == (pch >> 4) * 15 + (pch & 15)) & ((pch & 15) != 15))
    moved = dot(rows_by_z, lat_ref[...]).astype(BF16)
    moved = dot(moved, spread) + pad_ref[...]
    latp[...] = moved.astype(BF16).reshape(16, 16, QP)
    wz[0, z] = wloc_ref[0]
    wz[1, z] = wloc_ref[1]
    pl.semaphore_wait(barrier, 15 + 7 + 6 + 4)

    def chain_send(l, d, i):
        if d == 0:
            block, to = (z + 17 - i) % 16, dev(x, y, zu, c)
        else:
            block, to = (z + i - 1) % 16, dev(x, y, zd, c)
        send(wz.at[l, block], wz.at[l, block], wz_s.at[l, d, i - 1], wz_r.at[l, d, i - 1], to)

    def chain_step(l, i):
        arrive(wz.at[l, (z + 16 - i) % 16], wz_r.at[l, 0, i - 1])
        if i < 8:
            chain_send(l, 0, i + 1)
            arrive(wz.at[l, (z + i) % 16], wz_r.at[l, 1, i - 1])
            if i < 7:
                chain_send(l, 1, i + 1)

    def scatter_send(l):
        for a in range(2):
            half = (x // 2 + a) % 2
            t = half * 2 + c
            for b in range(2):
                j = (c + b) % 2
                src = wz.at[l, pl.ds(half * 8, 8), j]
                dst = wf.at[l, y, x]
                copy = pltpu.make_async_remote_copy(
                    src_ref=src, dst_ref=dst, send_sem=wx_s.at[l, a * 2 + b], recv_sem=wx_r.at[l, x],
                    device_id=dev(t, y, z, j), device_id_type=MESH,
                )
                if a == 0 and b == 0:
                    own = pltpu.make_async_copy(src, dst, wx_r.at[l, x])

                    @pl.when(c == x % 2)
                    def _():
                        own.start()

                    @pl.when(c != x % 2)
                    def _():
                        copy.start()

                    scattered.append(copy)
                else:
                    copy.start()
                    sends.append(copy)

    scattered = []

    def piece(l, yy, xx):
        return wf.at[l, yy, xx]

    def ring_send(l):
        for p in range(4):
            arrive(piece(l, y, p), wx_r.at[l, p])
            for d, to in ((0, yu), (1, yd)):
                send(piece(l, y, p), piece(l, y, p), wy_s.at[l, d, p], wy_r.at[l, d, p], dev(x, to, z, c))

    def ring_forward(l):
        for p in range(4):
            arrive(piece(l, yd, p), wy_r.at[l, 0, p])
            if p < 2:
                send(piece(l, yd, p), piece(l, yd, p), wg_s.at[l, p], wg_r.at[l, p], dev(x, yu, z, c))
            arrive(piece(l, yu, p), wy_r.at[l, 1, p])
            if p >= 2:
                send(piece(l, yu, p), piece(l, yu, p), wg_s.at[l, p], wg_r.at[l, p], dev(x, yd, z, c))

    def ring_end(l):
        for p in range(4):
            arrive(piece(l, yo, p), wg_r.at[l, p])
        send(wf.at[l, :, :, :, :, pl.ds(384, 128)], wos.at[l], wo_s.at[l], wo_r.at[l], dev(x, y, z, 1 - c))

    chain_send(0, 0, 1)
    chain_send(0, 1, 1)
    own_z = pltpu.make_async_copy(latp.at[z], r1.at[z], az_r.at[0])
    own_z.start()
    for o in range(1, 16):
        to = (z + o) % 16
        send(latp.at[to], r1.at[z], az_s.at[o], az_r.at[o], dev(x, y, to, c))

    for i in range(1, 9):
        chain_step(0, i)
    scatter_send(0)

    own_z.wait()
    for o in range(1, 16):
        arrive(r1.at[(z + 16 - o) % 16], az_r.at[o])
    rows_by_y = onehot(col == ((row >> 1) & 15) * 16 + (row >> 5) * 2 + (row & 1))
    y1[...] = dot(rows_by_y, r1[...].reshape(256, QP)).astype(BF16).reshape(8, 2, 16, QP)
    own_y = pltpu.make_async_copy(y1.at[y * 2 + c], xq.at[:, c, y], ay_r.at[0])
    own_y.start()
    for o in range(4):
        for j in range(2):
            if o or j:
                to, par = (y + o) % 4, (c + j) % 2
                send(
                    y1.at[to * 2 + par], xq.at[:, c, y], ay_s.at[o * 2 + j], ay_r.at[o * 2 + j],
                    dev(x, to, z, par),
                )
    chain_send(1, 0, 1)
    chain_send(1, 1, 1)
    ring_send(0)

    own_y.wait()
    for o in range(4):
        for j in range(2):
            if o or j:
                arrive(xq.at[:, (c + j) % 2, (y + 4 - o) % 4], ay_r.at[o * 2 + j])
    for h in range(4):
        resid[:, h * QP:(h + 1) * QP] = xq[h // 2, h % 2].reshape(64, QP).astype(F32)

    real = (iota((1, DP), 1) & 15) != 15

    def norm_rows(l):
        rows = resid[...]
        square = jnp.where(real, rows * rows, 0.0)
        mean_square = jnp.sum(square, axis=1, keepdims=True) * (1.0 / D)
        normed = jnp.where(real, rows * lax.rsqrt(mean_square + EPSILON) * gain_ref[l], rows)
        xn[l, c, x] = normed.astype(BF16).reshape(4, 16, DP)

    def gather_send(l):
        mine = xn.at[l, c, x]
        send(mine, mine, ag_s.at[l, 0], ag_r.at[l, 0], dev(xu, y, z, c))
        send(mine, mine, ag_s.at[l, 1], ag_r.at[l, 1], dev(xd, y, z, c))
        send(mine, mine, ag_s.at[l, 2], ag_r.at[l, 2], dev(x, y, z, 1 - c))

    def gather_forward(l):
        sibling = dev(x, y, z, 1 - c)
        low, high = pl.ds(0, 2), pl.ds(2, 2)
        block = xn.at[l, c, xd]
        arrive(block, ag_r.at[l, 0])
        send(xn.at[l, c, xd, low], xn.at[l, c, xd, low], ag_s.at[l, 3], ag_r.at[l, 3], dev(xu, y, z, c))
        send(block, block, ag_s.at[l, 4], ag_r.at[l, 4], sibling)
        block = xn.at[l, c, xu]
        arrive(block, ag_r.at[l, 1])
        send(xn.at[l, c, xu, high], xn.at[l, c, xu, high], ag_s.at[l, 5], ag_r.at[l, 5], dev(xd, y, z, c))
        send(block, block, ag_s.at[l, 6], ag_r.at[l, 6], sibling)

    def gather_end(l):
        sibling = dev(x, y, z, 1 - c)
        low, high = pl.ds(0, 2), pl.ds(2, 2)
        for part, got, to in ((low, 3, 7), (high, 5, 8)):
            block = xn.at[l, c, xo, part]
            arrive(block, ag_r.at[l, got])
            send(block, block, ag_s.at[l, to], ag_r.at[l, to], sibling)
        arrive(xn.at[l, 1 - c, x], ag_r.at[l, 2])
        arrive(xn.at[l, 1 - c, xd], ag_r.at[l, 4])
        arrive(xn.at[l, 1 - c, xu], ag_r.at[l, 6])
        arrive(xn.at[l, 1 - c, xo, low], ag_r.at[l, 7])
        arrive(xn.at[l, 1 - c, xo, high], ag_r.at[l, 8])

    def project(l):
        weight = wf[l].reshape(DP, QP)[:, :384]
        for p in range(2):
            qkv[p] = dot(xn[l, p].reshape(256, DP), weight).astype(BF16)

    lane = iota((1, 128), 1)
    frame = iota((1, 256), 1) & 1

    def first_frame(p):
        tile = xn[0, p, clip_x, y, :, :128].astype(F32)
        spot = (iota((16, 128), 0) == (pair * 2 + p) * 2) & (iota((16, 128), 1) == 15)
        kept = jnp.where(spot, tile, 0.0)
        return jnp.sum(jnp.sum(kept, axis=1, keepdims=True), axis=0, keepdims=True)

    def attend(p, prev_keys, prev_values, visible):
        queries = qkv[p, :, :128] * jnp.asarray(0.125, BF16)
        keys, values = qkv[p, :, 128:256], qkv[p, :, 256:384]
        parts = []
        for hh in range(2):
            mine = (lane // 64) == hh
            q = jnp.where(mine, queries, jnp.zeros_like(queries))
            own = dot_t(q, keys)
            past = jnp.where(visible, dot_t(q, prev_keys), -jnp.inf)
            highest = jnp.maximum(jnp.max(own, axis=1, keepdims=True), jnp.max(past, axis=1, keepdims=True))
            own, past = jnp.exp(own - highest), jnp.exp(past - highest)
            scale = 1.0 / (jnp.sum(own, axis=1, keepdims=True) + jnp.sum(past, axis=1, keepdims=True))
            parts.append(
                dot((own * scale).astype(BF16), values) + dot((past * scale).astype(BF16), prev_values)
            )
        return jnp.where(lane < 64, parts[0], parts[1]).astype(BF16)

    gather_like = pl.ds(128, 256)
    norm_rows(0)
    gather_send(0)
    ring_forward(0)
    gather_forward(0)
    gather_end(0)
    ring_end(0)
    starts = [first_frame(p) for p in range(2)]

    for l in range(LAYERS):
        project(l)
        send(qkv.at[1, :, gather_like], pkv.at[l], kv_s.at[l], kv_r.at[l], dev(x, y, zu, c))
        see = frame.astype(F32) >= starts[1]
        blb[1] = attend(1, qkv[0, :, 128:256], qkv[0, :, 256:384], see)
        if l == 0:
            for i in range(1, 9):
                chain_step(1, i)
            scatter_send(1)
        arrive(pkv.at[l], kv_r.at[l])
        see = (frame.astype(F32) >= starts[0]) & (pair > 0)
        blb[0] = attend(0, pkv[l, :, :128], pkv[l, :, 128:], see)
        send(blb.at[1 - c], bls.at[l], bl_s.at[l], bl_r.at[l], dev(x, y, z, 1 - c))
        if l == 0:
            ring_send(1)
        arrive(bls.at[l], bl_r.at[l])
        arrive(wos.at[l], wo_r.at[l])
        blended = jnp.concatenate([blb[c], bls[l]], axis=1)
        weight = jnp.concatenate([wf[l, :, :, :, :, 384:], wos[l]], axis=4).reshape(DP, 256)
        gs[l] = dot_t(blended, weight).astype(BF16).reshape(4, 64, DP)
        for o in range(1, 4):
            to = (x + o) % 4
            send(gs.at[l, to], rsb.at[l, o - 1], rs_s.at[l, o - 1], rs_r.at[l, o - 1], dev(to, y, z, c))
        if l == 0:
            ring_forward(1)
        for o in range(1, 4):
            arrive(rsb.at[l, o - 1], rs_r.at[l, o - 1])
        total = gs[l, x].astype(F32) + rsb[l, 0].astype(F32) + rsb[l, 1].astype(F32) + rsb[l, 2].astype(F32)
        resid[...] += total
        if l == 0:
            norm_rows(1)
            gather_send(1)
            drain_upto = len(sends)
            gather_forward(1)
            gather_end(1)
            ring_end(1)
            for copy in sends[:drain_upto]:
                copy.wait_send()
            del sends[:drain_upto]

    refined = resid[...].astype(BF16)
    for b in range(D // 128):
        first = ((b * 128 // 15) * 16 + (b * 128) % 15) // 128 * 128
        width = min(384, DP - first)
        a, ch = iota((width, 128), 0) + first, iota((width, 128), 1) + b * 128
        group = (ch * 4370) >> 16
        pick = onehot(a == group * 16 + (ch - group * 15))
        fo[:, :, b * 128:(b + 1) * 128] = dot(refined[:, first:first + width], pick).astype(BF16).reshape(4, 16, 128)
    last = []
    stretch = pair * 2 + c
    for q in range(4):
        to_z = stretch + 8 * (q // 2)
        copy = pltpu.make_async_remote_copy(
            src_ref=fo.at[q], dst_ref=out_ref.at[x], send_sem=fi_s.at[q], recv_sem=fi_r.at[x],
            device_id=dev(clip_x, y, to_z, q % 2), device_id_type=MESH,
        )
        own = pltpu.make_async_copy(fo.at[q], out_ref.at[x], fi_r.at[x])
        here = (clip_x == x) & (to_z == z) & (c == q % 2)
        last.append((copy, here))

        @pl.when(here)
        def _():
            own.start()

        @pl.when(jnp.logical_not(here))
        def _():
            copy.start()

    for p in range(4):
        arrive(out_ref.at[p], fi_r.at[p])
    for copy, here in last:

        @pl.when(jnp.logical_not(here))
        def _():
            copy.wait_send()

    for copy in scattered:

        @pl.when(c != x % 2)
        def _():
            copy.wait_send()

    for copy in sends:
        copy.wait_send()


def local(latent, start_frame, norm_gains, qkv_weight, out_weight):
    pad_row = jnp.where(jnp.arange(QP) % 16 == 15, start_frame[0].astype(F32), 0.0)[None, :]
    gains = jnp.pad(norm_gains.reshape(LAYERS, 128, 15), ((0, 0), (0, 0), (0, 1))).reshape(LAYERS, 1, DP)
    both = jnp.concatenate([qkv_weight, out_weight.transpose(0, 2, 1)[:, :, None, :]], axis=2)
    both = both.reshape(LAYERS, 15, 4, 2, 128).transpose(0, 3, 1, 2, 4).reshape(LAYERS, 2, 15, QP)
    both = jnp.pad(both, ((0, 0), (0, 0), (0, 1), (0, 0)))
    dma = pltpu.SemaphoreType.DMA
    vmem = pltpu.VMEM
    out = pl.pallas_call(
        kernel,
        out_shape=jax.ShapeDtypeStruct((4, 16, D), BF16),
        in_specs=[pl.BlockSpec(memory_space=vmem)] * 4,
        out_specs=pl.BlockSpec(memory_space=vmem),
        scratch_shapes=[
            vmem((16, 16, QP), BF16),
            vmem((16, 16, QP), BF16),
            vmem((8, 2, 16, QP), BF16),
            vmem((2, 2, 4, 16, QP), BF16),
            vmem((LAYERS, 16, 2, 16, QP), BF16),
            vmem((LAYERS, 4, 4, 8, 16, QP), BF16),
            vmem((LAYERS, 4, 4, 8, 16, 128), BF16),
            vmem((64, DP), F32),
            vmem((LAYERS, 2, 4, 4, 16, DP), BF16),
            vmem((2, 256, 384), BF16),
            vmem((LAYERS, 256, 256), BF16),
            vmem((2, 256, 128), BF16),
            vmem((LAYERS, 256, 128), BF16),
            vmem((LAYERS, 4, 64, DP), BF16),
            vmem((LAYERS, 3, 64, DP), BF16),
            vmem((4, 16, D), BF16),
            dma((16,)), dma((16,)), dma((8,)), dma((8,)),
            dma((LAYERS, 2, 8)), dma((LAYERS, 2, 8)), dma((LAYERS, 4)), dma((LAYERS, 4)),
            dma((LAYERS, 2, 4)), dma((LAYERS, 2, 4)), dma((LAYERS, 4)), dma((LAYERS, 4)),
            dma((LAYERS,)), dma((LAYERS,)), dma((LAYERS, 9)), dma((LAYERS, 9)),
            dma((LAYERS,)), dma((LAYERS,)), dma((LAYERS,)), dma((LAYERS,)),
            dma((LAYERS, 3)), dma((LAYERS, 3)), dma((4,)), dma((4,)),
        ],
        compiler_params=pltpu.CompilerParams(
            collective_id=0, has_side_effects=True, vmem_limit_bytes=56 * 2**20
        ),
    )(latent[0], pad_row, gains, both)
    return out.reshape(32, 2, D)


def solution(mesh):
    return jax.shard_map(
        local,
        mesh=mesh,
        in_specs=(
            P("tm", None, "head"),
            P("tm"),
            P(),
            P(None, "tm", None, "head"),
            P(None, "head", "tm"),
        ),
        out_specs=P("head", "tm", None),
        check_vma=False,
    )
```

```python
import jax
import jax.numpy as jnp
from jax import lax
from jax.experimental import pallas as pl
from jax.experimental.pallas import tpu as pltpu
from jax.sharding import PartitionSpec as P

NX, NY, NZ, ZLO = 4, 4, 16, 8
LAYERS = 2
D = 1920
DP = 2048
QP = 512
EPSILON = 1e-06
F32, BF16 = jnp.float32, jnp.bfloat16
MESH = pl.DeviceIdType.MESH


def dot(a, b):
    return jnp.dot(a, b, preferred_element_type=F32)


def dot_t(a, b):
    return lax.dot_general(a, b, (((1,), (1,)), ((), ())), preferred_element_type=F32)


def iota(shape, dim):
    return lax.broadcasted_iota(jnp.int32, shape, dim)


def onehot(mask):
    return jnp.where(mask, 1.0, 0.0).astype(BF16)


def kernel(
    lat_ref, pad_ref, gain_ref, wloc_ref, out_ref,
    latp, r1, y1, xq, wz, wf, wos, resid, xn, qkv, pkv, blb, bls, gs, rsb, rst, rso, fo,
    az_s, az_r, ay_s, ay_r, wz_s, wz_r, wx_s, wx_r, wy_s, wy_r, wg_s, wg_r,
    wo_s, wo_r, ag_s, ag_r, kv_s, kv_r, bl_s, bl_r, rs_s, rs_r, fi_s, fi_r,
):
    tm, hd = lax.axis_index("tm"), lax.axis_index("head")
    y, x, zl = tm // 32, (tm // 8) % 4, tm % 8
    zh, c = hd // 2, hd % 2
    z = zh * 8 + zl

    def dev(xx, yy, zz, cc):
        return (yy * 32 + xx * 8 + zz % 8, (zz // 8) * 2 + cc)

    sends = []

    def send(src, dst, s_sem, r_sem, to):
        copy = pltpu.make_async_remote_copy(
            src_ref=src, dst_ref=dst, send_sem=s_sem, recv_sem=r_sem,
            device_id=to, device_id_type=MESH,
        )
        copy.start()
        sends.append(copy)

    def arrive(dst, sem):
        pltpu.make_async_copy(dst, dst, sem).wait()

    clip_x = z // 4
    pair = z % 4
    xu, xd, xo = (x + 1) % 4, (x + 3) % 4, (x + 2) % 4
    yu, yd, yo = (y + 1) % 4, (y + 3) % 4, (y + 2) % 4
    zu, zd = (z + 1) % 16, (z + 15) % 16

    barrier = pltpu.get_barrier_semaphore()

    def greet(to):
        pl.semaphore_signal(barrier, inc=1, device_id=to, device_id_type=MESH)

    for o in range(1, 16):
        greet(dev(x, y, (z + o) % 16, c))
    for o in range(4):
        for j in range(2):
            if o or j:
                greet(dev((x + o) % 4, y, z, (c + j) % 2))
    for o in range(1, 4):
        for j in range(2):
            greet(dev(x, (y + o) % 4, z, (c + j) % 2))
    for o in range(4):
        greet(dev((x + o) % 4, y, x * 4 + zl // 2, zl % 2))

    row, col = iota((256, 256), 0), iota((256, 256), 1)
    rows_by_z = onehot(col == ((row >> 2) & 3) * 64 + (row >> 4) * 4 + (row & 3))
    chan, pch = iota((480, QP), 0), iota((480, QP), 1)
    spread = onehot((chan == (pch >> 4) * 15 + (pch & 15)) & ((pch & 15) != 15))
    moved = dot(rows_by_z, lat_ref[...]).astype(BF16)
    moved = dot(moved, spread) + pad_ref[...]
    latp[...] = moved.astype(BF16).reshape(16, 16, QP)
    wz[0, z] = wloc_ref[0]
    wz[1, z] = wloc_ref[1]
    pl.semaphore_wait(barrier, 15 + 7 + 6 + 4)

    def chain_send(l, d, i):
        if d == 0:
            block, to = (z + 17 - i) % 16, dev(x, y, zu, c)
        else:
            block, to = (z + i - 1) % 16, dev(x, y, zd, c)
        send(wz.at[l, block], wz.at[l, block], wz_s.at[l, d, i - 1], wz_r.at[l, d, i - 1], to)

    def chain_step(l, i):
        arrive(wz.at[l, (z + 16 - i) % 16], wz_r.at[l, 0, i - 1])
        if i < 8:
            chain_send(l, 0, i + 1)
            arrive(wz.at[l, (z + i) % 16], wz_r.at[l, 1, i - 1])
            if i < 7:
                chain_send(l, 1, i + 1)

    def scatter_send(l):
        for a in range(2):
            half = (x // 2 + a) % 2
            t = half * 2 + c
            for b in range(2):
                j = (c + b) % 2
                src = wz.at[l, pl.ds(half * 8, 8), j]
                dst = wf.at[l, y, x]
                copy = pltpu.make_async_remote_copy(
                    src_ref=src, dst_ref=dst, send_sem=wx_s.at[l, a * 2 + b], recv_sem=wx_r.at[l, x],
                    device_id=dev(t, y, z, j), device_id_type=MESH,
                )
                if a == 0 and b == 0:
                    own = pltpu.make_async_copy(src, dst, wx_r.at[l, x])

                    @pl.when(c == x % 2)
                    def _():
                        own.start()

                    @pl.when(c != x % 2)
                    def _():
                        copy.start()

                    scattered.append(copy)
                else:
                    copy.start()
                    sends.append(copy)

    scattered = []

    def piece(l, yy, xx):
        return wf.at[l, yy, xx]

    def lanes(l, yy, xx, part):
        return wf.at[l, yy, xx, :, :, pl.ds(0, 384) if part == 0 else pl.ds(384, 128)]

    def ring_send(l, part):
        for p in range(4):
            if part == 0:
                arrive(piece(l, y, p), wx_r.at[l, p])
            block = lanes(l, y, p, part)
            for d, to in ((0, yu), (1, yd)):
                send(block, block, wy_s.at[l, part, d, p], wy_r.at[l, part, d, p], dev(x, to, z, c))

    def ring_forward(l, part, p):
        below, above = lanes(l, yd, p, part), lanes(l, yu, p, part)
        arrive(below, wy_r.at[l, part, 0, p])
        if p < 2:
            send(below, below, wg_s.at[l, part, p], wg_r.at[l, part, p], dev(x, yu, z, c))
        arrive(above, wy_r.at[l, part, 1, p])
        if p >= 2:
            send(above, above, wg_s.at[l, part, p], wg_r.at[l, part, p], dev(x, yd, z, c))

    def ring_end(l, part):
        for p in range(4):
            arrive(lanes(l, yo, p, part), wg_r.at[l, part, p])
        if part == 1:
            send(wf.at[l, :, :, :, :, pl.ds(384, 128)], wos.at[l], wo_s.at[l], wo_r.at[l], dev(x, y, z, 1 - c))

    chain_send(0, 0, 1)
    chain_send(0, 1, 1)
    own_z = pltpu.make_async_copy(latp.at[z], r1.at[z], az_r.at[0])
    own_z.start()

    def latent_send(o):
        to = (z + o) % 16
        send(latp.at[to], r1.at[z], az_s.at[o], az_r.at[o], dev(x, y, to, c))

    for i in range(1, 9):
        latent_send(9 - i)
        if i > 1:
            latent_send(7 + i)
        chain_step(0, i)
    scatter_send(0)
    chain_send(1, 0, 1)
    chain_send(1, 1, 1)

    own_z.wait()
    for o in range(1, 16):
        arrive(r1.at[(z + 16 - o) % 16], az_r.at[o])
    rows_by_y = onehot(col == ((row >> 1) & 15) * 16 + (row >> 5) * 2 + (row & 1))
    y1[...] = dot(rows_by_y, r1[...].reshape(256, QP)).astype(BF16).reshape(8, 2, 16, QP)
    own_y = pltpu.make_async_copy(y1.at[y * 2 + c], xq.at[:, c, y], ay_r.at[0])
    own_y.start()
    for o in range(4):
        for j in range(2):
            if o or j:
                to, par = (y + o) % 4, (c + j) % 2
                send(
                    y1.at[to * 2 + par], xq.at[:, c, y], ay_s.at[o * 2 + j], ay_r.at[o * 2 + j],
                    dev(x, to, z, par),
                )
    chain_step(1, 1)
    ring_send(0, 0)
    chain_step(1, 2)

    own_y.wait()
    for o in range(4):
        for j in range(2):
            if o or j:
                arrive(xq.at[:, (c + j) % 2, (y + 4 - o) % 4], ay_r.at[o * 2 + j])
    for h in range(4):
        resid[:, h * QP:(h + 1) * QP] = xq[h // 2, h % 2].reshape(64, QP).astype(F32)

    real = (iota((1, DP), 1) & 15) != 15

    def norm_rows(l):
        rows = resid[...]
        square = jnp.where(real, rows * rows, 0.0)
        mean_square = jnp.sum(square, axis=1, keepdims=True) * (1.0 / D)
        normed = jnp.where(real, rows * lax.rsqrt(mean_square + EPSILON) * gain_ref[l], rows)
        xn[l, c, x] = normed.astype(BF16).reshape(4, 16, DP)

    low, high = pl.ds(0, 2), pl.ds(2, 2)

    def gather_copy(l, block, n, to):
        send(block, block, ag_s.at[l, n], ag_r.at[l, n], to)

    def gather_send(l):
        up, down = dev(xu, y, z, c), dev(xd, y, z, c)
        gather_copy(l, xn.at[l, c, x, low], 0, up)
        gather_copy(l, xn.at[l, c, x, high], 1, down)
        gather_copy(l, xn.at[l, c, x, high], 2, up)
        gather_copy(l, xn.at[l, c, x, low], 3, down)
        gather_copy(l, xn.at[l, c, x], 4, dev(x, y, z, 1 - c))

    def gather_forward(l):
        arrive(xn.at[l, c, xd, low], ag_r.at[l, 0])
        gather_copy(l, xn.at[l, c, xd, low], 5, dev(xu, y, z, c))
        arrive(xn.at[l, c, xu, high], ag_r.at[l, 1])
        gather_copy(l, xn.at[l, c, xu, high], 6, dev(xd, y, z, c))

    def gather_sides(l):
        sibling = dev(x, y, z, 1 - c)
        arrive(xn.at[l, c, xd, high], ag_r.at[l, 2])
        gather_copy(l, xn.at[l, c, xd], 7, sibling)
        arrive(xn.at[l, c, xu, low], ag_r.at[l, 3])
        gather_copy(l, xn.at[l, c, xu], 8, sibling)

    def gather_far(l):
        sibling = dev(x, y, z, 1 - c)
        arrive(xn.at[l, c, xo, low], ag_r.at[l, 5])
        gather_copy(l, xn.at[l, c, xo, low], 9, sibling)
        arrive(xn.at[l, c, xo, high], ag_r.at[l, 6])
        gather_copy(l, xn.at[l, c, xo, high], 10, sibling)

    def gather_end(l):
        arrive(xn.at[l, 1 - c, x], ag_r.at[l, 4])
        arrive(xn.at[l, 1 - c, xd], ag_r.at[l, 7])
        arrive(xn.at[l, 1 - c, xu], ag_r.at[l, 8])
        arrive(xn.at[l, 1 - c, xo, low], ag_r.at[l, 9])
        arrive(xn.at[l, 1 - c, xo, high], ag_r.at[l, 10])

    def project(l):
        weight = wf[l, :, :, :, :, :384].reshape(DP, 384)
        qkv[c] = dot(xn[l, c].reshape(256, DP), weight).astype(BF16)
        gather_end(l)
        qkv[1 - c] = dot(xn[l, 1 - c].reshape(256, DP), weight).astype(BF16)

    lane = iota((1, 128), 1)
    frame = iota((1, 256), 1) & 1

    def first_frame(p):
        tile = xn[0, p, clip_x, y, :, :128].astype(F32)
        spot = (iota((16, 128), 0) == (pair * 2 + p) * 2) & (iota((16, 128), 1) == 15)
        kept = jnp.where(spot, tile, 0.0)
        return jnp.sum(jnp.sum(kept, axis=1, keepdims=True), axis=0, keepdims=True)

    def attend(p, prev_keys, prev_values, visible):
        queries = qkv[p, :, :128] * jnp.asarray(0.125, BF16)
        keys, values = qkv[p, :, 128:256], qkv[p, :, 256:384]
        parts = []
        for hh in range(2):
            mine = (lane // 64) == hh
            q = jnp.where(mine, queries, jnp.zeros_like(queries))
            own = dot_t(q, keys)
            past = jnp.where(visible, dot_t(q, prev_keys), -jnp.inf)
            highest = jnp.maximum(jnp.max(own, axis=1, keepdims=True), jnp.max(past, axis=1, keepdims=True))
            own, past = jnp.exp(own - highest), jnp.exp(past - highest)
            scale = 1.0 / (jnp.sum(own, axis=1, keepdims=True) + jnp.sum(past, axis=1, keepdims=True))
            parts.append(
                dot((own * scale).astype(BF16), values) + dot((past * scale).astype(BF16), prev_values)
            )
        return jnp.where(lane < 64, parts[0], parts[1]).astype(BF16)

    gather_like = pl.ds(128, 256)
    norm_rows(0)
    gather_send(0)
    chain_step(1, 3)
    ring_forward(0, 0, 0)
    gather_forward(0)
    chain_step(1, 4)
    ring_forward(0, 0, 1)
    gather_sides(0)
    chain_step(1, 5)
    ring_forward(0, 0, 2)
    gather_far(0)
    chain_step(1, 6)
    ring_forward(0, 0, 3)
    ring_send(0, 1)
    chain_step(1, 7)
    chain_step(1, 8)
    scatter_send(1)
    ring_end(0, 0)

    for l in range(LAYERS):
        project(l)
        send(qkv.at[1, :, gather_like], pkv.at[l], kv_s.at[l], kv_r.at[l], dev(x, y, zu, c))
        if l == 0:
            starts = [first_frame(p) for p in range(2)]
        see = frame.astype(F32) >= starts[1]
        blb[1] = attend(1, qkv[0, :, 128:256], qkv[0, :, 256:384], see).reshape(4, 64, 128)
        if l == 0:
            for p in range(4):
                ring_forward(0, 1, p)
            ring_send(1, 0)
        arrive(pkv.at[l], kv_r.at[l])
        see = (frame.astype(F32) >= starts[0]) & (pair > 0)
        blb[0] = attend(0, pkv[l, :, :128], pkv[l, :, 128:], see).reshape(4, 64, 128)
        send(blb.at[1 - c], bls.at[l], bl_s.at[l], bl_r.at[l], dev(x, y, z, 1 - c))
        if l == 0:
            ring_end(0, 1)
        arrive(bls.at[l], bl_r.at[l])
        arrive(wos.at[l], wo_r.at[l])
        weight = jnp.concatenate([wf[l, :, :, :, :, 384:], wos[l]], axis=4).reshape(DP, 256)

        def update(to):
            blended = jnp.concatenate([blb[c, to], bls[l, to]], axis=1)
            gs[l, to] = dot_t(blended, weight).astype(BF16)

        up, down = dev(xu, y, z, c), dev(xd, y, z, c)
        first, second = pl.ds(0, 32), pl.ds(32, 32)

        def scatter_copy(src, dst, n, to):
            send(src, dst, rs_s.at[l, n], rs_r.at[l, n], to)

        update(xo)
        scatter_copy(gs.at[l, xo, first], rst.at[l, 0], 0, up)
        scatter_copy(gs.at[l, xo, second], rst.at[l, 1], 1, down)
        update(xu)
        scatter_copy(gs.at[l, xu, second], rsb.at[l, 0, second], 2, up)
        update(xd)
        scatter_copy(gs.at[l, xd, first], rsb.at[l, 1, first], 3, down)
        arrive(rst.at[l, 0], rs_r.at[l, 0])
        rso[l, 0] = (gs[l, xu, :32].astype(F32) + rst[l, 0].astype(F32)).astype(BF16)
        scatter_copy(rso.at[l, 0], rsb.at[l, 0, first], 4, up)
        arrive(rst.at[l, 1], rs_r.at[l, 1])
        rso[l, 1] = (gs[l, xd, 32:].astype(F32) + rst[l, 1].astype(F32)).astype(BF16)
        scatter_copy(rso.at[l, 1], rsb.at[l, 1, second], 5, down)
        update(x)
        if l == 0:
            for p in range(4):
                ring_forward(1, 0, p)
            ring_send(1, 1)
        arrive(rsb.at[l, 0, second], rs_r.at[l, 2])
        arrive(rsb.at[l, 1, first], rs_r.at[l, 3])
        arrive(rsb.at[l, 0, first], rs_r.at[l, 4])
        arrive(rsb.at[l, 1, second], rs_r.at[l, 5])
        resid[...] += gs[l, x].astype(F32) + rsb[l, 0].astype(F32) + rsb[l, 1].astype(F32)
        if l == 0:
            norm_rows(1)
            gather_send(1)
            drain_upto = len(sends)
            gather_forward(1)
            gather_sides(1)
            for copy in sends[:drain_upto]:
                copy.wait_send()
            del sends[:drain_upto]
            gather_far(1)
            for p in range(4):
                ring_forward(1, 1, p)
            ring_end(1, 0)
            ring_end(1, 1)

    refined = resid[...].astype(BF16)
    for b in range(D // 128):
        first = ((b * 128 // 15) * 16 + (b * 128) % 15) // 128 * 128
        width = min(384, DP - first)
        a, ch = iota((width, 128), 0) + first, iota((width, 128), 1) + b * 128
        group = (ch * 4370) >> 16
        pick = onehot(a == group * 16 + (ch - group * 15))
        fo[:, :, b * 128:(b + 1) * 128] = dot(refined[:, first:first + width], pick).astype(BF16).reshape(4, 16, 128)
    last = []
    stretch = pair * 2 + c
    for q in range(4):
        to_z = stretch + 8 * (q // 2)
        copy = pltpu.make_async_remote_copy(
            src_ref=fo.at[q], dst_ref=out_ref.at[x], send_sem=fi_s.at[q], recv_sem=fi_r.at[x],
            device_id=dev(clip_x, y, to_z, q % 2), device_id_type=MESH,
        )
        own = pltpu.make_async_copy(fo.at[q], out_ref.at[x], fi_r.at[x])
        here = (clip_x == x) & (to_z == z) & (c == q % 2)
        last.append((copy, here))

        @pl.when(here)
        def _():
            own.start()

        @pl.when(jnp.logical_not(here))
        def _():
            copy.start()

    for p in range(4):
        arrive(out_ref.at[p], fi_r.at[p])
    for copy, here in last:

        @pl.when(jnp.logical_not(here))
        def _():
            copy.wait_send()

    for copy in scattered:

        @pl.when(c != x % 2)
        def _():
            copy.wait_send()

    for copy in sends:
        copy.wait_send()


def local(latent, start_frame, norm_gains, qkv_weight, out_weight):
    pad_row = jnp.where(jnp.arange(QP) % 16 == 15, start_frame[0].astype(F32), 0.0)[None, :]
    gains = jnp.pad(norm_gains.reshape(LAYERS, 128, 15), ((0, 0), (0, 0), (0, 1))).reshape(LAYERS, 1, DP)
    both = jnp.concatenate([qkv_weight, out_weight.transpose(0, 2, 1)[:, :, None, :]], axis=2)
    both = both.reshape(LAYERS, 15, 4, 2, 128).transpose(0, 3, 1, 2, 4).reshape(LAYERS, 2, 15, QP)
    both = jnp.pad(both, ((0, 0), (0, 0), (0, 1), (0, 0)))
    dma = pltpu.SemaphoreType.DMA
    vmem = pltpu.VMEM
    out = pl.pallas_call(
        kernel,
        out_shape=jax.ShapeDtypeStruct((4, 16, D), BF16),
        in_specs=[pl.BlockSpec(memory_space=vmem)] * 4,
        out_specs=pl.BlockSpec(memory_space=vmem),
        scratch_shapes=[
            vmem((16, 16, QP), BF16),
            vmem((16, 16, QP), BF16),
            vmem((8, 2, 16, QP), BF16),
            vmem((2, 2, 4, 16, QP), BF16),
            vmem((LAYERS, 16, 2, 16, QP), BF16),
            vmem((LAYERS, 4, 4, 8, 16, QP), BF16),
            vmem((LAYERS, 4, 4, 8, 16, 128), BF16),
            vmem((64, DP), F32),
            vmem((LAYERS, 2, 4, 4, 16, DP), BF16),
            vmem((2, 256, 384), BF16),
            vmem((LAYERS, 256, 256), BF16),
            vmem((2, 4, 64, 128), BF16),
            vmem((LAYERS, 4, 64, 128), BF16),
            vmem((LAYERS, 4, 64, DP), BF16),
            vmem((LAYERS, 2, 64, DP), BF16),
            vmem((LAYERS, 2, 32, DP), BF16),
            vmem((LAYERS, 2, 32, DP), BF16),
            vmem((4, 16, D), BF16),
            dma((16,)), dma((16,)), dma((8,)), dma((8,)),
            dma((LAYERS, 2, 8)), dma((LAYERS, 2, 8)), dma((LAYERS, 4)), dma((LAYERS, 4)),
            dma((LAYERS, 2, 2, 4)), dma((LAYERS, 2, 2, 4)), dma((LAYERS, 2, 4)), dma((LAYERS, 2, 4)),
            dma((LAYERS,)), dma((LAYERS,)), dma((LAYERS, 11)), dma((LAYERS, 11)),
            dma((LAYERS,)), dma((LAYERS,)), dma((LAYERS,)), dma((LAYERS,)),
            dma((LAYERS, 6)), dma((LAYERS, 6)), dma((4,)), dma((4,)),
        ],
        compiler_params=pltpu.CompilerParams(
            collective_id=0, has_side_effects=True, vmem_limit_bytes=56 * 2**20
        ),
    )(latent[0], pad_row, gains, both)
    return out.reshape(32, 2, D)


def solution(mesh):
    return jax.shard_map(
        local,
        mesh=mesh,
        in_specs=(
            P("tm", None, "head"),
            P("tm"),
            P(),
            P(None, "tm", None, "head"),
            P(None, "head", "tm"),
        ),
        out_specs=P("head", "tm", None),
        check_vma=False,
    )
```

```python
import jax
import jax.numpy as jnp
from jax import lax
from jax.experimental import pallas as pl
from jax.experimental.pallas import tpu as pltpu
from jax.sharding import PartitionSpec as P

NX, NY, NZ, ZLO = 4, 4, 16, 8
LAYERS = 2
D = 1920
DP = 2048
QP = 512
EPSILON = 1e-06
F32, BF16 = jnp.float32, jnp.bfloat16
MESH = pl.DeviceIdType.MESH


def dot(a, b):
    return jnp.dot(a, b, preferred_element_type=F32)


def dot_t(a, b):
    return lax.dot_general(a, b, (((1,), (1,)), ((), ())), preferred_element_type=F32)


def iota(shape, dim):
    return lax.broadcasted_iota(jnp.int32, shape, dim)


def onehot(mask):
    return jnp.where(mask, 1.0, 0.0).astype(BF16)


def kernel(
    lat_ref, start_ref, gain_ref, wloc_ref, out_ref,
    gains, latp, r1, y1, xq, wz, wf, wos, resid, xn, qkv, pkv, blb, bls, gs, rsb, rst, rso, fo,
    az_s, az_r, ay_s, ay_r, wz_s, wz_r, wx_s, wx_r, wy_s, wy_r, wg_s, wg_r,
    wo_s, wo_r, ag_s, ag_r, kv_s, kv_r, bl_s, bl_r, rs_s, rs_r, fi_s, fi_r,
):
    tm, hd = lax.axis_index("tm"), lax.axis_index("head")
    y, x, zl = tm // 32, (tm // 8) % 4, tm % 8
    zh, c = hd // 2, hd % 2
    z = zh * 8 + zl

    def dev(xx, yy, zz, cc):
        return (yy * 32 + xx * 8 + zz % 8, (zz // 8) * 2 + cc)

    sends = []

    def send(src, dst, s_sem, r_sem, to):
        copy = pltpu.make_async_remote_copy(
            src_ref=src, dst_ref=dst, send_sem=s_sem, recv_sem=r_sem,
            device_id=to, device_id_type=MESH,
        )
        copy.start()
        sends.append(copy)

    def arrive(dst, sem):
        pltpu.make_async_copy(dst, dst, sem).wait()

    clip_x = z // 4
    pair = z % 4
    xu, xd, xo = (x + 1) % 4, (x + 3) % 4, (x + 2) % 4
    yu, yd, yo = (y + 1) % 4, (y + 3) % 4, (y + 2) % 4
    zu, zd = (z + 1) % 16, (z + 15) % 16

    barrier = pltpu.get_barrier_semaphore()

    def greet(to):
        pl.semaphore_signal(barrier, inc=1, device_id=to, device_id_type=MESH)

    for o in range(1, 16):
        greet(dev(x, y, (z + o) % 16, c))
    for o in range(4):
        for j in range(2):
            if o or j:
                greet(dev((x + o) % 4, y, z, (c + j) % 2))
    for o in range(1, 4):
        for j in range(2):
            greet(dev(x, (y + o) % 4, z, (c + j) % 2))
    for o in range(4):
        greet(dev((x + o) % 4, y, x * 4 + zl // 2, zl % 2))

    row, col = iota((256, 256), 0), iota((256, 256), 1)
    rows_by_z = onehot(col == ((row >> 2) & 3) * 64 + (row >> 4) * 4 + (row & 3))
    chan, pch = iota((480, QP), 0), iota((480, QP), 1)
    spread = onehot((chan == (pch >> 4) * 15 + (pch & 15)) & ((pch & 15) != 15))
    moved = dot_t(rows_by_z, lat_ref[...]).astype(BF16)
    pad_row = jnp.where((iota((1, QP), 1) & 15) == 15, start_ref[0].astype(F32), 0.0)
    moved = dot(moved, spread) + pad_row
    latp[...] = moved.astype(BF16).reshape(16, 16, QP)
    wz[0, z] = wloc_ref[0]
    wz[1, z] = wloc_ref[1]
    pl.semaphore_wait(barrier, 15 + 7 + 6 + 4)

    reach = (8, 7)

    def chain_send(l, d, block, hop, k):
        to = dev(x, y, (z + hop) % 16 if d == 0 else (z + 16 - hop) % 16, c)
        send(wz.at[l, block], wz.at[l, block], wz_s.at[l, d, k - 1], wz_r.at[l, d, k - 1], to)

    def chain_start(l):
        for k in (1, 2):
            for d in range(2):
                chain_send(l, d, z, k, k)
        scatter_block(l, z, 0)

    def chain_step(l, i):
        for k in (2 * i - 1, 2 * i):
            for d in range(2):
                if k <= reach[d]:
                    block = (z + 16 - k) % 16 if d == 0 else (z + k) % 16
                    arrive(wz.at[l, block], wz_r.at[l, d, k - 1])
                    if k + 2 <= reach[d]:
                        chain_send(l, d, block, 2, k + 2)
                    scatter_block(l, block, k if d == 0 else 8 + k)

    def scatter_block(l, block, n):
        half, at = block // 8, block % 8
        t = half * 2 + c
        for b in range(2):
            j = (c + b) % 2
            src, dst = wz.at[l, block, j], wf.at[l, y, x, at]
            copy = pltpu.make_async_remote_copy(
                src_ref=src, dst_ref=dst, send_sem=wx_s.at[l, n, b], recv_sem=wx_r.at[l, x],
                device_id=dev(t, y, z, j), device_id_type=MESH,
            )
            if b == 0:
                own = pltpu.make_async_copy(src, dst, wx_r.at[l, x])

                @pl.when(t == x)
                def _():
                    own.start()

                @pl.when(t != x)
                def _():
                    copy.start()

                scattered.append((copy, t))
            else:
                copy.start()
                sends.append(copy)

    scattered = []

    def piece(l, yy, xx):
        return wf.at[l, yy, xx]

    def lanes(l, yy, xx, part):
        return wf.at[l, yy, xx, :, :, pl.ds(0, 384) if part == 0 else pl.ds(384, 128)]

    def ring_send(l, part):
        for p in range(4):
            if part == 0:
                arrive(piece(l, y, p), wx_r.at[l, p])
            block = lanes(l, y, p, part)
            for d, to in ((0, yu), (1, yd)):
                send(block, block, wy_s.at[l, part, d, p], wy_r.at[l, part, d, p], dev(x, to, z, c))

    def ring_forward(l, part, p):
        below, above = lanes(l, yd, p, part), lanes(l, yu, p, part)
        arrive(below, wy_r.at[l, part, 0, p])
        if p < 2:
            send(below, below, wg_s.at[l, part, p], wg_r.at[l, part, p], dev(x, yu, z, c))
        arrive(above, wy_r.at[l, part, 1, p])
        if p >= 2:
            send(above, above, wg_s.at[l, part, p], wg_r.at[l, part, p], dev(x, yd, z, c))

    def ring_end(l, part):
        for p in range(4):
            arrive(lanes(l, yo, p, part), wg_r.at[l, part, p])
        if part == 1:
            send(wf.at[l, :, :, :, :, pl.ds(384, 128)], wos.at[l], wo_s.at[l], wo_r.at[l], dev(x, y, z, 1 - c))

    chain_start(0)
    own_z = pltpu.make_async_copy(latp.at[z], r1.at[z], az_r.at[0])
    own_z.start()

    def latent_send(o):
        to = (z + o) % 16
        send(latp.at[to], r1.at[z], az_s.at[o], az_r.at[o], dev(x, y, to, c))

    order = ((8, 7, 9, 6), (10, 5, 11, 4), (12, 3, 13, 2), (14, 1, 15))
    for i in range(1, 5):
        for o in order[i - 1]:
            latent_send(o)
        chain_step(0, i)
    rest, split = gain_ref[...], []
    for _ in range(3):
        split.append(rest.astype(BF16))
        rest = rest - split[-1].astype(F32)
    split = jnp.concatenate(split, axis=0)
    for q in range(4):
        base = q * 480 // 128 * 128
        width = min(640, D - base)
        chan, pch = iota((width, QP), 0) + (base - q * 480), iota((width, QP), 1)
        pick = onehot((chan == (pch >> 4) * 15 + (pch & 15)) & ((pch & 15) != 15))
        parts = dot(split[:, base:base + width], pick)
        gains[:, q * QP:(q + 1) * QP] = parts[:2] + parts[2:4] + parts[4:]
    chain_start(1)

    own_z.wait()
    for o in range(1, 16):
        arrive(r1.at[(z + 16 - o) % 16], az_r.at[o])
    rows_by_y = onehot(col == ((row >> 1) & 15) * 16 + (row >> 5) * 2 + (row & 1))
    y1[...] = dot(rows_by_y, r1[...].reshape(256, QP)).astype(BF16).reshape(8, 2, 16, QP)
    own_y = pltpu.make_async_copy(y1.at[y * 2 + c], xq.at[:, c, y], ay_r.at[0])
    own_y.start()
    for o in range(4):
        for j in range(2):
            if o or j:
                to, par = (y + o) % 4, (c + j) % 2
                send(
                    y1.at[to * 2 + par], xq.at[:, c, y], ay_s.at[o * 2 + j], ay_r.at[o * 2 + j],
                    dev(x, to, z, par),
                )
    chain_step(1, 1)
    ring_send(0, 0)
    chain_step(1, 2)

    own_y.wait()
    for o in range(4):
        for j in range(2):
            if o or j:
                arrive(xq.at[:, (c + j) % 2, (y + 4 - o) % 4], ay_r.at[o * 2 + j])
    for h in range(4):
        resid[:, h * QP:(h + 1) * QP] = xq[h // 2, h % 2].reshape(64, QP).astype(F32)

    real = (iota((1, DP), 1) & 15) != 15

    def norm_rows(l):
        rows = resid[...]
        square = jnp.where(real, rows * rows, 0.0)
        mean_square = jnp.sum(square, axis=1, keepdims=True) * (1.0 / D)
        normed = jnp.where(real, rows * lax.rsqrt(mean_square + EPSILON) * gains[l:l + 1], rows)
        xn[l, c, x] = normed.astype(BF16).reshape(4, 16, DP)

    low, high = pl.ds(0, 2), pl.ds(2, 2)

    def gather_copy(l, block, n, to):
        send(block, block, ag_s.at[l, n], ag_r.at[l, n], to)

    def gather_send(l):
        up, down = dev(xu, y, z, c), dev(xd, y, z, c)
        gather_copy(l, xn.at[l, c, x, low], 0, up)
        gather_copy(l, xn.at[l, c, x, high], 1, down)
        gather_copy(l, xn.at[l, c, x, high], 2, up)
        gather_copy(l, xn.at[l, c, x, low], 3, down)
        gather_copy(l, xn.at[l, c, x], 4, dev(x, y, z, 1 - c))

    def gather_forward(l):
        arrive(xn.at[l, c, xd, low], ag_r.at[l, 0])
        gather_copy(l, xn.at[l, c, xd, low], 5, dev(xu, y, z, c))
        arrive(xn.at[l, c, xu, high], ag_r.at[l, 1])
        gather_copy(l, xn.at[l, c, xu, high], 6, dev(xd, y, z, c))

    def gather_sides(l):
        sibling = dev(x, y, z, 1 - c)
        arrive(xn.at[l, c, xd, high], ag_r.at[l, 2])
        gather_copy(l, xn.at[l, c, xd], 7, sibling)
        arrive(xn.at[l, c, xu, low], ag_r.at[l, 3])
        gather_copy(l, xn.at[l, c, xu], 8, sibling)

    def gather_far(l):
        sibling = dev(x, y, z, 1 - c)
        arrive(xn.at[l, c, xo, low], ag_r.at[l, 5])
        gather_copy(l, xn.at[l, c, xo, low], 9, sibling)
        arrive(xn.at[l, c, xo, high], ag_r.at[l, 6])
        gather_copy(l, xn.at[l, c, xo, high], 10, sibling)

    def gather_end(l):
        arrive(xn.at[l, 1 - c, x], ag_r.at[l, 4])
        arrive(xn.at[l, 1 - c, xd], ag_r.at[l, 7])
        arrive(xn.at[l, 1 - c, xu], ag_r.at[l, 8])
        arrive(xn.at[l, 1 - c, xo, low], ag_r.at[l, 9])
        arrive(xn.at[l, 1 - c, xo, high], ag_r.at[l, 10])

    def project(l):
        weight = wf[l, :, :, :, :, :384].reshape(DP, 384)
        qkv[c] = dot(xn[l, c].reshape(256, DP), weight).astype(BF16)
        gather_end(l)
        qkv[1 - c] = dot(xn[l, 1 - c].reshape(256, DP), weight).astype(BF16)

    lane = iota((1, 128), 1)
    frame = iota((1, 256), 1) & 1

    def first_frame(p):
        tile = xn[0, p, clip_x, y, :, :128].astype(F32)
        spot = (iota((16, 128), 0) == (pair * 2 + p) * 2) & (iota((16, 128), 1) == 15)
        kept = jnp.where(spot, tile, 0.0)
        return jnp.sum(jnp.sum(kept, axis=1, keepdims=True), axis=0, keepdims=True)

    def attend(p, prev_keys, prev_values, visible):
        queries = qkv[p, :, :128] * jnp.asarray(0.125, BF16)
        keys, values = qkv[p, :, 128:256], qkv[p, :, 256:384]
        parts = []
        for hh in range(2):
            mine = (lane // 64) == hh
            q = jnp.where(mine, queries, jnp.zeros_like(queries))
            own = dot_t(q, keys)
            past = jnp.where(visible, dot_t(q, prev_keys), -jnp.inf)
            highest = jnp.maximum(jnp.max(own, axis=1, keepdims=True), jnp.max(past, axis=1, keepdims=True))
            own, past = jnp.exp(own - highest), jnp.exp(past - highest)
            scale = 1.0 / (jnp.sum(own, axis=1, keepdims=True) + jnp.sum(past, axis=1, keepdims=True))
            parts.append(
                dot((own * scale).astype(BF16), values) + dot((past * scale).astype(BF16), prev_values)
            )
        return jnp.where(lane < 64, parts[0], parts[1]).astype(BF16)

    gather_like = pl.ds(128, 256)
    norm_rows(0)
    gather_send(0)
    chain_step(1, 3)
    ring_forward(0, 0, 0)
    gather_forward(0)
    ring_forward(0, 0, 1)
    gather_sides(0)
    chain_step(1, 4)
    ring_forward(0, 0, 2)
    gather_far(0)
    ring_forward(0, 0, 3)
    ring_send(0, 1)
    ring_end(0, 0)

    for l in range(LAYERS):
        project(l)
        send(qkv.at[1, :, gather_like], pkv.at[l], kv_s.at[l], kv_r.at[l], dev(x, y, zu, c))
        if l == 0:
            starts = [first_frame(p) for p in range(2)]
        see = frame.astype(F32) >= starts[1]
        blb[1] = attend(1, qkv[0, :, 128:256], qkv[0, :, 256:384], see).reshape(4, 64, 128)
        if l == 0:
            for p in range(4):
                ring_forward(0, 1, p)
            ring_send(1, 0)
        arrive(pkv.at[l], kv_r.at[l])
        see = (frame.astype(F32) >= starts[0]) & (pair > 0)
        blb[0] = attend(0, pkv[l, :, :128], pkv[l, :, 128:], see).reshape(4, 64, 128)
        send(blb.at[1 - c], bls.at[l], bl_s.at[l], bl_r.at[l], dev(x, y, z, 1 - c))
        if l == 0:
            ring_end(0, 1)
        arrive(bls.at[l], bl_r.at[l])
        arrive(wos.at[l], wo_r.at[l])
        weight = jnp.concatenate([wf[l, :, :, :, :, 384:], wos[l]], axis=4).reshape(DP, 256)

        def update(to):
            blended = jnp.concatenate([blb[c, to], bls[l, to]], axis=1)
            gs[l, to] = dot_t(blended, weight).astype(BF16)

        up, down = dev(xu, y, z, c), dev(xd, y, z, c)
        first, second = pl.ds(0, 32), pl.ds(32, 32)

        def scatter_copy(src, dst, n, to):
            send(src, dst, rs_s.at[l, n], rs_r.at[l, n], to)

        update(xo)
        scatter_copy(gs.at[l, xo, first], rst.at[l, 0], 0, up)
        scatter_copy(gs.at[l, xo, second], rst.at[l, 1], 1, down)
        update(xu)
        scatter_copy(gs.at[l, xu, second], rsb.at[l, 0, second], 2, up)
        update(xd)
        scatter_copy(gs.at[l, xd, first], rsb.at[l, 1, first], 3, down)
        arrive(rst.at[l, 0], rs_r.at[l, 0])
        rso[l, 0] = (gs[l, xu, :32].astype(F32) + rst[l, 0].astype(F32)).astype(BF16)
        scatter_copy(rso.at[l, 0], rsb.at[l, 0, first], 4, up)
        arrive(rst.at[l, 1], rs_r.at[l, 1])
        rso[l, 1] = (gs[l, xd, 32:].astype(F32) + rst[l, 1].astype(F32)).astype(BF16)
        scatter_copy(rso.at[l, 1], rsb.at[l, 1, second], 5, down)
        update(x)
        if l == 0:
            for p in range(4):
                ring_forward(1, 0, p)
            ring_send(1, 1)
        arrive(rsb.at[l, 0, second], rs_r.at[l, 2])
        arrive(rsb.at[l, 1, first], rs_r.at[l, 3])
        arrive(rsb.at[l, 0, first], rs_r.at[l, 4])
        arrive(rsb.at[l, 1, second], rs_r.at[l, 5])
        resid[...] += gs[l, x].astype(F32) + rsb[l, 0].astype(F32) + rsb[l, 1].astype(F32)
        if l == 0:
            norm_rows(1)
            gather_send(1)
            drain_upto = len(sends)
            gather_forward(1)
            gather_sides(1)
            for copy in sends[:drain_upto]:
                copy.wait_send()
            del sends[:drain_upto]
            gather_far(1)
            for p in range(4):
                ring_forward(1, 1, p)
            ring_end(1, 0)
            ring_end(1, 1)

    refined = resid[...].astype(BF16)
    for b in range(D // 128):
        first = ((b * 128 // 15) * 16 + (b * 128) % 15) // 128 * 128
        width = min(384, DP - first)
        a, ch = iota((width, 128), 0) + first, iota((width, 128), 1) + b * 128
        group = (ch * 4370) >> 16
        pick = onehot(a == group * 16 + (ch - group * 15))
        fo[:, :, b * 128:(b + 1) * 128] = dot(refined[:, first:first + width], pick).astype(BF16).reshape(4, 16, 128)
    last = []
    stretch = pair * 2 + c
    for q in range(4):
        to_z = stretch + 8 * (q // 2)
        copy = pltpu.make_async_remote_copy(
            src_ref=fo.at[q], dst_ref=out_ref.at[x], send_sem=fi_s.at[q], recv_sem=fi_r.at[x],
            device_id=dev(clip_x, y, to_z, q % 2), device_id_type=MESH,
        )
        own = pltpu.make_async_copy(fo.at[q], out_ref.at[x], fi_r.at[x])
        here = (clip_x == x) & (to_z == z) & (c == q % 2)
        last.append((copy, here))

        @pl.when(here)
        def _():
            own.start()

        @pl.when(jnp.logical_not(here))
        def _():
            copy.start()

    for p in range(4):
        arrive(out_ref.at[p], fi_r.at[p])
    for copy, here in last:

        @pl.when(jnp.logical_not(here))
        def _():
            copy.wait_send()

    for copy, t in scattered:

        @pl.when(t != x)
        def _():
            copy.wait_send()

    for copy in sends:
        copy.wait_send()


def local(latent, start_frame, norm_gains, qkv_weight, out_weight):
    both = jnp.concatenate([qkv_weight, out_weight.transpose(0, 2, 1)[:, :, None, :]], axis=2)
    both = both.reshape(LAYERS, 15, 4, 2, 128).transpose(0, 3, 1, 2, 4).reshape(LAYERS, 2, 15, QP)
    both = jnp.pad(both, ((0, 0), (0, 0), (0, 1), (0, 0)))
    dma = pltpu.SemaphoreType.DMA
    vmem = pltpu.VMEM
    out = pl.pallas_call(
        kernel,
        out_shape=jax.ShapeDtypeStruct((4, 16, D), BF16),
        in_specs=[
            pl.BlockSpec(memory_space=vmem),
            pl.BlockSpec(memory_space=pltpu.SMEM),
            pl.BlockSpec(memory_space=vmem),
            pl.BlockSpec(memory_space=vmem),
        ],
        out_specs=pl.BlockSpec(memory_space=vmem),
        scratch_shapes=[
            vmem((LAYERS, DP), F32),
            vmem((16, 16, QP), BF16),
            vmem((16, 16, QP), BF16),
            vmem((8, 2, 16, QP), BF16),
            vmem((2, 2, 4, 16, QP), BF16),
            vmem((LAYERS, 16, 2, 16, QP), BF16),
            vmem((LAYERS, 4, 4, 8, 16, QP), BF16),
            vmem((LAYERS, 4, 4, 8, 16, 128), BF16),
            vmem((64, DP), F32),
            vmem((LAYERS, 2, 4, 4, 16, DP), BF16),
            vmem((2, 256, 384), BF16),
            vmem((LAYERS, 256, 256), BF16),
            vmem((2, 4, 64, 128), BF16),
            vmem((LAYERS, 4, 64, 128), BF16),
            vmem((LAYERS, 4, 64, DP), BF16),
            vmem((LAYERS, 2, 64, DP), BF16),
            vmem((LAYERS, 2, 32, DP), BF16),
            vmem((LAYERS, 2, 32, DP), BF16),
            vmem((4, 16, D), BF16),
            dma((16,)), dma((16,)), dma((8,)), dma((8,)),
            dma((LAYERS, 2, 8)), dma((LAYERS, 2, 8)), dma((LAYERS, 16, 2)), dma((LAYERS, 4)),
            dma((LAYERS, 2, 2, 4)), dma((LAYERS, 2, 2, 4)), dma((LAYERS, 2, 4)), dma((LAYERS, 2, 4)),
            dma((LAYERS,)), dma((LAYERS,)), dma((LAYERS, 11)), dma((LAYERS, 11)),
            dma((LAYERS,)), dma((LAYERS,)), dma((LAYERS,)), dma((LAYERS,)),
            dma((LAYERS, 6)), dma((LAYERS, 6)), dma((4,)), dma((4,)),
        ],
        compiler_params=pltpu.CompilerParams(
            collective_id=0, has_side_effects=True, vmem_limit_bytes=56 * 2**20
        ),
    )(latent[0].T, start_frame, norm_gains, both)
    return out.reshape(32, 2, D)


def solution(mesh):
    return jax.shard_map(
        local,
        mesh=mesh,
        in_specs=(
            P("tm", None, "head"),
            P("tm"),
            P(),
            P(None, "tm", None, "head"),
            P(None, "head", "tm"),
        ),
        out_specs=P("head", "tm", None),
        check_vma=False,
    )
```

```python
import jax
import jax.numpy as jnp
from jax import lax
from jax.experimental import pallas as pl
from jax.experimental.pallas import tpu as pltpu
from jax.sharding import PartitionSpec as P

NX, NY, NZ, ZLO = 4, 4, 16, 8
LAYERS = 2
D = 1920
DP = 2048
QP = 512
EPSILON = 1e-06
F32, BF16 = jnp.float32, jnp.bfloat16
MESH = pl.DeviceIdType.MESH


def dot(a, b):
    return jnp.dot(a, b, preferred_element_type=F32)


def dot_t(a, b):
    return lax.dot_general(a, b, (((1,), (1,)), ((), ())), preferred_element_type=F32)


def iota(shape, dim):
    return lax.broadcasted_iota(jnp.int32, shape, dim)


def onehot(mask):
    return jnp.where(mask, 1.0, 0.0).astype(BF16)


def kernel(
    lat_ref, start_ref, gain_ref, wloc_ref, out_ref,
    gains, latp, r1, y1, xq, wz, wf, wos, resid, xn, qkv, pkv, blb, bls, gs, rsb, rst, rso, fo, pick,
    az_s, az_r, ay_s, ay_r, wz_s, wz_r, wx_s, wx_r, wy_s, wy_r, wg_s, wg_r,
    wo_s, wo_r, ag_s, ag_r, kv_s, kv_r, bl_s, bl_r, rs_s, rs_r, fi_s, fi_r,
):
    tm, hd = lax.axis_index("tm"), lax.axis_index("head")
    y, x, zl = tm // 32, (tm // 8) % 4, tm % 8
    zh, c = hd // 2, hd % 2
    z = zh * 8 + zl

    def dev(xx, yy, zz, cc):
        return (yy * 32 + xx * 8 + zz % 8, (zz // 8) * 2 + cc)

    sends = []

    def send(src, dst, s_sem, r_sem, to):
        copy = pltpu.make_async_remote_copy(
            src_ref=src, dst_ref=dst, send_sem=s_sem, recv_sem=r_sem,
            device_id=to, device_id_type=MESH,
        )
        copy.start()
        sends.append(copy)

    def arrive(dst, sem):
        pltpu.make_async_copy(dst, dst, sem).wait()

    clip_x = z // 4
    pair = z % 4
    xu, xd, xo = (x + 1) % 4, (x + 3) % 4, (x + 2) % 4
    yu, yd, yo = (y + 1) % 4, (y + 3) % 4, (y + 2) % 4
    zu, zd = (z + 1) % 16, (z + 15) % 16

    barrier = pltpu.get_barrier_semaphore()

    def greet(to):
        pl.semaphore_signal(barrier, inc=1, device_id=to, device_id_type=MESH)

    for o in range(1, 16):
        greet(dev(x, y, (z + o) % 16, c))
    for o in range(4):
        for j in range(2):
            if o or j:
                greet(dev((x + o) % 4, y, z, (c + j) % 2))
    for o in range(1, 4):
        for j in range(2):
            greet(dev(x, (y + o) % 4, z, (c + j) % 2))
    for o in range(4):
        greet(dev((x + o) % 4, y, x * 4 + zl // 2, zl % 2))

    row, col = iota((256, 256), 0), iota((256, 256), 1)
    rows_by_z = onehot(col == ((row >> 2) & 3) * 64 + (row >> 4) * 4 + (row & 3))
    chan, pch = iota((480, QP), 0), iota((480, QP), 1)
    spread = onehot((chan == (pch >> 4) * 15 + (pch & 15)) & ((pch & 15) != 15))
    moved = dot_t(rows_by_z, lat_ref[...]).astype(BF16)
    pad_row = jnp.where((iota((1, QP), 1) & 15) == 15, start_ref[0].astype(F32), 0.0)
    moved = dot(moved, spread) + pad_row
    latp[...] = moved.astype(BF16).reshape(16, 16, QP)
    wz[0, z] = wloc_ref[0]
    wz[1, z] = wloc_ref[1]
    pl.semaphore_wait(barrier, 15 + 7 + 6 + 4)

    reach = (8, 7)

    def chain_send(l, d, block, hop, k):
        to = dev(x, y, (z + hop) % 16 if d == 0 else (z + 16 - hop) % 16, c)
        send(wz.at[l, block], wz.at[l, block], wz_s.at[l, d, k - 1], wz_r.at[l, d, k - 1], to)

    def chain_start(l):
        for k in (1, 2):
            for d in range(2):
                chain_send(l, d, z, k, k)
        scatter_block(l, z, 0)

    def chain_step(l, i):
        for k in (2 * i - 1, 2 * i):
            for d in range(2):
                if k <= reach[d]:
                    block = (z + 16 - k) % 16 if d == 0 else (z + k) % 16
                    arrive(wz.at[l, block], wz_r.at[l, d, k - 1])
                    if k + 2 <= reach[d]:
                        chain_send(l, d, block, 2, k + 2)
                    scatter_block(l, block, k if d == 0 else 8 + k)

    def scatter_block(l, block, n):
        half, at = block // 8, block % 8
        t = half * 2 + c
        for b in range(2):
            j = (c + b) % 2
            src, dst = wz.at[l, block, j], wf.at[l, y, x, at]
            copy = pltpu.make_async_remote_copy(
                src_ref=src, dst_ref=dst, send_sem=wx_s.at[l, n, b], recv_sem=wx_r.at[l, x],
                device_id=dev(t, y, z, j), device_id_type=MESH,
            )
            if b == 0:
                own = pltpu.make_async_copy(src, dst, wx_r.at[l, x])

                @pl.when(t == x)
                def _():
                    own.start()

                @pl.when(t != x)
                def _():
                    copy.start()

                scattered.append((copy, t))
            else:
                copy.start()
                sends.append(copy)

    scattered = []

    def piece(l, yy, xx):
        return wf.at[l, yy, xx]

    def lanes(l, yy, xx, part):
        return wf.at[l, yy, xx, :, :, pl.ds(0, 384) if part == 0 else pl.ds(384, 128)]

    def ring_send(l, part):
        for p in range(4):
            if part == 0:
                arrive(piece(l, y, p), wx_r.at[l, p])
            block = lanes(l, y, p, part)
            for d, to in ((0, yu), (1, yd)):
                send(block, block, wy_s.at[l, part, d, p], wy_r.at[l, part, d, p], dev(x, to, z, c))

    def ring_forward(l, part, p):
        below, above = lanes(l, yd, p, part), lanes(l, yu, p, part)
        arrive(below, wy_r.at[l, part, 0, p])
        if p < 2:
            send(below, below, wg_s.at[l, part, p], wg_r.at[l, part, p], dev(x, yu, z, c))
        arrive(above, wy_r.at[l, part, 1, p])
        if p >= 2:
            send(above, above, wg_s.at[l, part, p], wg_r.at[l, part, p], dev(x, yd, z, c))

    def ring_end(l, part):
        for p in range(4):
            arrive(lanes(l, yo, p, part), wg_r.at[l, part, p])
        if part == 1:
            send(wf.at[l, :, :, :, :, pl.ds(384, 128)], wos.at[l], wo_s.at[l], wo_r.at[l], dev(x, y, z, 1 - c))

    chain_start(0)
    own_z = pltpu.make_async_copy(latp.at[z], r1.at[z], az_r.at[0])
    own_z.start()

    def latent_send(o):
        to = (z + o) % 16
        send(latp.at[to], r1.at[z], az_s.at[o], az_r.at[o], dev(x, y, to, c))

    order = ((8, 7, 9, 6), (10, 5, 11, 4), (12, 3, 13, 2), (14, 1, 15))
    for i in range(1, 5):
        for o in order[i - 1]:
            latent_send(o)
        chain_step(0, i)
    rest, split = gain_ref[...], []
    for _ in range(3):
        split.append(rest.astype(BF16))
        rest = rest - split[-1].astype(F32)
    split = jnp.concatenate(split, axis=0)
    for q in range(4):
        base = q * 480 // 128 * 128
        width = min(640, D - base)
        chan, pch = iota((width, QP), 0) + (base - q * 480), iota((width, QP), 1)
        chosen = onehot((chan == (pch >> 4) * 15 + (pch & 15)) & ((pch & 15) != 15))
        parts = dot(split[:, base:base + width], chosen)
        gains[:, q * QP:(q + 1) * QP] = parts[:2] + parts[2:4] + parts[4:]
    chain_start(1)

    own_z.wait()
    for o in range(1, 16):
        arrive(r1.at[(z + 16 - o) % 16], az_r.at[o])
    rows_by_y = onehot(col == ((row >> 1) & 15) * 16 + (row >> 5) * 2 + (row & 1))
    y1[...] = dot(rows_by_y, r1[...].reshape(256, QP)).astype(BF16).reshape(8, 2, 16, QP)
    own_y = pltpu.make_async_copy(y1.at[y * 2 + c], xq.at[:, c, y], ay_r.at[0])
    own_y.start()
    for o in range(4):
        for j in range(2):
            if o or j:
                to, par = (y + o) % 4, (c + j) % 2
                send(
                    y1.at[to * 2 + par], xq.at[:, c, y], ay_s.at[o * 2 + j], ay_r.at[o * 2 + j],
                    dev(x, to, z, par),
                )
    chain_step(1, 1)
    ring_send(0, 0)
    chain_step(1, 2)

    own_y.wait()
    for o in range(4):
        for j in range(2):
            if o or j:
                arrive(xq.at[:, (c + j) % 2, (y + 4 - o) % 4], ay_r.at[o * 2 + j])
    for h in range(4):
        resid[:, h * QP:(h + 1) * QP] = xq[h // 2, h % 2].reshape(64, QP).astype(F32)

    real = (iota((1, DP), 1) & 15) != 15

    def quarter(q):
        return slice(q * 16, (q + 1) * 16)

    def norm_rows(l, q):
        rows = resid[quarter(q)]
        square = jnp.where(real, rows * rows, 0.0)
        mean_square = jnp.sum(square, axis=1, keepdims=True) * (1.0 / D)
        normed = jnp.where(real, rows * lax.rsqrt(mean_square + EPSILON) * gains[l:l + 1], rows)
        xn[l, c, x, q] = normed.astype(BF16)

    def gather_copy(l, block, n, k, to):
        send(block, block, ag_s.at[l, n, k], ag_r.at[l, n, k], to)

    def gather_send(l, k):
        up, down = dev(xu, y, z, c), dev(xd, y, z, c)
        gather_copy(l, xn.at[l, c, x, k], 0, k, up)
        gather_copy(l, xn.at[l, c, x, 2 + k], 1, k, down)
        gather_copy(l, xn.at[l, c, x, 2 + k], 2, k, up)
        gather_copy(l, xn.at[l, c, x, k], 3, k, down)
        if k == 1:
            gather_copy(l, xn.at[l, c, x], 4, 0, dev(x, y, z, 1 - c))

    def gather_forward(l, k):
        arrive(xn.at[l, c, xd, k], ag_r.at[l, 0, k])
        gather_copy(l, xn.at[l, c, xd, k], 5, k, dev(xu, y, z, c))
        arrive(xn.at[l, c, xu, 2 + k], ag_r.at[l, 1, k])
        gather_copy(l, xn.at[l, c, xu, 2 + k], 6, k, dev(xd, y, z, c))

    def gather_sides(l):
        sibling = dev(x, y, z, 1 - c)
        for k in range(2):
            arrive(xn.at[l, c, xd, 2 + k], ag_r.at[l, 2, k])
        gather_copy(l, xn.at[l, c, xd], 7, 0, sibling)
        for k in range(2):
            arrive(xn.at[l, c, xu, k], ag_r.at[l, 3, k])
        gather_copy(l, xn.at[l, c, xu], 8, 0, sibling)

    def gather_far(l):
        sibling = dev(x, y, z, 1 - c)
        for k in range(2):
            arrive(xn.at[l, c, xo, k], ag_r.at[l, 5, k])
            gather_copy(l, xn.at[l, c, xo, k], 9, k, sibling)
            arrive(xn.at[l, c, xo, 2 + k], ag_r.at[l, 6, k])
            gather_copy(l, xn.at[l, c, xo, 2 + k], 10, k, sibling)

    def gather_end(l):
        arrive(xn.at[l, 1 - c, x], ag_r.at[l, 4, 0])
        arrive(xn.at[l, 1 - c, xd], ag_r.at[l, 7, 0])
        arrive(xn.at[l, 1 - c, xu], ag_r.at[l, 8, 0])
        for k in range(2):
            arrive(xn.at[l, 1 - c, xo, k], ag_r.at[l, 9, k])
            arrive(xn.at[l, 1 - c, xo, 2 + k], ag_r.at[l, 10, k])

    def project(l):
        weight = wf[l, :, :, :, :, :384].reshape(DP, 384)
        qkv[c] = dot(xn[l, c].reshape(256, DP), weight).astype(BF16)
        gather_end(l)
        qkv[1 - c] = dot(xn[l, 1 - c].reshape(256, DP), weight).astype(BF16)

    lane = iota((1, 128), 1)
    frame = iota((1, 256), 1) & 1

    def first_frame(p):
        tile = xn[0, p, clip_x, y, :, :128].astype(F32)
        spot = (iota((16, 128), 0) == (pair * 2 + p) * 2) & (iota((16, 128), 1) == 15)
        kept = jnp.where(spot, tile, 0.0)
        return jnp.sum(jnp.sum(kept, axis=1, keepdims=True), axis=0, keepdims=True)

    def attend(p, prev_keys, prev_values, visible):
        queries = qkv[p, :, :128] * jnp.asarray(0.125, BF16)
        keys, values = qkv[p, :, 128:256], qkv[p, :, 256:384]
        parts = []
        for hh in range(2):
            mine = (lane // 64) == hh
            q = jnp.where(mine, queries, jnp.zeros_like(queries))
            own = dot_t(q, keys)
            past = jnp.where(visible, dot_t(q, prev_keys), -jnp.inf)
            highest = jnp.maximum(jnp.max(own, axis=1, keepdims=True), jnp.max(past, axis=1, keepdims=True))
            own, past = jnp.exp(own - highest), jnp.exp(past - highest)
            scale = 1.0 / (jnp.sum(own, axis=1, keepdims=True) + jnp.sum(past, axis=1, keepdims=True))
            parts.append(
                dot((own * scale).astype(BF16), values) + dot((past * scale).astype(BF16), prev_values)
            )
        return jnp.where(lane < 64, parts[0], parts[1]).astype(BF16)

    gather_like = pl.ds(128, 256)
    for k in range(2):
        norm_rows(0, k)
        norm_rows(0, 2 + k)
        gather_send(0, k)
    chain_step(1, 3)
    gather_forward(0, 0)
    ring_forward(0, 0, 0)
    gather_forward(0, 1)
    ring_forward(0, 0, 1)
    gather_sides(0)
    chain_step(1, 4)
    ring_forward(0, 0, 2)
    gather_far(0)
    ring_forward(0, 0, 3)
    ring_send(0, 1)
    ring_end(0, 0)

    def drop_pads():
        for b in range(D // 128):
            first, width = window(b)
            a, ch = iota((width, 128), 0) + first, iota((width, 128), 1) + b * 128
            group = (ch * 4370) >> 16
            pick[b, :width] = onehot(a == group * 16 + (ch - group * 15))

    def window(b):
        first = ((b * 128 // 15) * 16 + (b * 128) % 15) // 128 * 128
        return first, min(384, DP - first)

    last = []
    stretch = pair * 2 + c

    def finish(k):
        refined = jnp.concatenate([resid[quarter(k)], resid[quarter(2 + k)]], axis=0).astype(BF16)
        for b in range(D // 128):
            first, width = window(b)
            packed = dot(refined[:, first:first + width], pick[b, :width]).astype(BF16)
            fo[k, :, b * 128:(b + 1) * 128] = packed[:16]
            fo[2 + k, :, b * 128:(b + 1) * 128] = packed[16:]
        for q in (k, 2 + k):
            to_z = stretch + 8 * (q // 2)
            copy = pltpu.make_async_remote_copy(
                src_ref=fo.at[q], dst_ref=out_ref.at[x], send_sem=fi_s.at[q], recv_sem=fi_r.at[x],
                device_id=dev(clip_x, y, to_z, q % 2), device_id_type=MESH,
            )
            own = pltpu.make_async_copy(fo.at[q], out_ref.at[x], fi_r.at[x])
            here = (clip_x == x) & (to_z == z) & (c == q % 2)
            last.append((copy, here))
            launch(copy, own, here)

    def launch(copy, own, here):
        @pl.when(here)
        def _():
            own.start()

        @pl.when(jnp.logical_not(here))
        def _():
            copy.start()

    for l in range(LAYERS):
        project(l)
        send(qkv.at[1, :, gather_like], pkv.at[l], kv_s.at[l], kv_r.at[l], dev(x, y, zu, c))
        if l == 0:
            starts = [first_frame(p) for p in range(2)]
        see = frame.astype(F32) >= starts[1]
        blb[1] = attend(1, qkv[0, :, 128:256], qkv[0, :, 256:384], see).reshape(4, 64, 128)
        for p in range(4):
            ring_forward(l, 1, p)
        if l == 0:
            ring_send(1, 0)
            drop_pads()
        arrive(pkv.at[l], kv_r.at[l])
        see = (frame.astype(F32) >= starts[0]) & (pair > 0)
        blb[0] = attend(0, pkv[l, :, :128], pkv[l, :, 128:], see).reshape(4, 64, 128)
        send(blb.at[1 - c], bls.at[l], bl_s.at[l], bl_r.at[l], dev(x, y, z, 1 - c))
        ring_end(l, 1)
        arrive(bls.at[l], bl_r.at[l])
        arrive(wos.at[l], wo_r.at[l])
        weight = jnp.concatenate([wf[l, :, :, :, :, 384:], wos[l]], axis=4).reshape(DP, 256)

        def update(to):
            blended = jnp.concatenate([blb[c, to], bls[l, to]], axis=1)
            gs[l, to] = dot_t(blended, weight).astype(BF16).reshape(4, 16, DP)

        up, down = dev(xu, y, z, c), dev(xd, y, z, c)

        def scatter_copy(src, dst, n, k, to):
            send(src, dst, rs_s.at[l, n, k], rs_r.at[l, n, k], to)

        def scatter_plain(k):
            scatter_copy(gs.at[l, xu, 2 + k], rsb.at[l, 0, 2 + k], 2, k, up)
            scatter_copy(gs.at[l, xd, k], rsb.at[l, 1, k], 3, k, down)

        def scatter_sum(k):
            arrive(rst.at[l, 0, k], rs_r.at[l, 0, k])
            rso[l, 0, k] = (gs[l, xu, k].astype(F32) + rst[l, 0, k].astype(F32)).astype(BF16)
            scatter_copy(rso.at[l, 0, k], rsb.at[l, 0, k], 4, k, up)
            arrive(rst.at[l, 1, k], rs_r.at[l, 1, k])
            rso[l, 1, k] = (gs[l, xd, 2 + k].astype(F32) + rst[l, 1, k].astype(F32)).astype(BF16)
            scatter_copy(rso.at[l, 1, k], rsb.at[l, 1, 2 + k], 5, k, down)

        update(xo)
        for k in range(2):
            scatter_copy(gs.at[l, xo, k], rst.at[l, 0, k], 0, k, up)
            scatter_copy(gs.at[l, xo, 2 + k], rst.at[l, 1, k], 1, k, down)
        update(xu)
        update(xd)
        scatter_plain(0)
        scatter_sum(0)
        scatter_plain(1)
        scatter_sum(1)
        update(x)
        if l == 0:
            ring_forward(1, 0, 0)
            ring_forward(1, 0, 1)
        drain_upto = len(sends)
        for k in range(2):
            arrive(rsb.at[l, 0, 2 + k], rs_r.at[l, 2, k])
            arrive(rsb.at[l, 1, k], rs_r.at[l, 3, k])
            arrive(rsb.at[l, 0, k], rs_r.at[l, 4, k])
            arrive(rsb.at[l, 1, 2 + k], rs_r.at[l, 5, k])
            for q in (k, 2 + k):
                total = gs[l, x, q].astype(F32) + rsb[l, 0, q].astype(F32) + rsb[l, 1, q].astype(F32)
                resid[quarter(q)] += total
                if l == 0:
                    norm_rows(1, q)
            if l == 0:
                gather_send(1, k)
            else:
                finish(k)
        if l == 0:
            gather_forward(1, 0)
            ring_forward(1, 0, 2)
            ring_forward(1, 0, 3)
            gather_forward(1, 1)
            ring_send(1, 1)
            gather_sides(1)
            for copy in sends[:drain_upto]:
                copy.wait_send()
            del sends[:drain_upto]
            gather_far(1)
            ring_end(1, 0)

    for p in range(4):
        arrive(out_ref.at[p], fi_r.at[p])

    def settle(copy, there):
        @pl.when(there)
        def _():
            copy.wait_send()

    for copy, here in last:
        settle(copy, jnp.logical_not(here))
    for copy, t in scattered:
        settle(copy, t != x)
    for copy in sends:
        copy.wait_send()


def local(latent, start_frame, norm_gains, qkv_weight, out_weight):
    both = jnp.concatenate([qkv_weight, out_weight.transpose(0, 2, 1)[:, :, None, :]], axis=2)
    both = both.reshape(LAYERS, 15, 4, 2, 128).transpose(0, 3, 1, 2, 4).reshape(LAYERS, 2, 15, QP)
    both = jnp.pad(both, ((0, 0), (0, 0), (0, 1), (0, 0)))
    dma = pltpu.SemaphoreType.DMA
    vmem = pltpu.VMEM
    out = pl.pallas_call(
        kernel,
        out_shape=jax.ShapeDtypeStruct((4, 16, D), BF16),
        in_specs=[
            pl.BlockSpec(memory_space=vmem),
            pl.BlockSpec(memory_space=pltpu.SMEM),
            pl.BlockSpec(memory_space=vmem),
            pl.BlockSpec(memory_space=vmem),
        ],
        out_specs=pl.BlockSpec(memory_space=vmem),
        scratch_shapes=[
            vmem((LAYERS, DP), F32),
            vmem((16, 16, QP), BF16),
            vmem((16, 16, QP), BF16),
            vmem((8, 2, 16, QP), BF16),
            vmem((2, 2, 4, 16, QP), BF16),
            vmem((LAYERS, 16, 2, 16, QP), BF16),
            vmem((LAYERS, 4, 4, 8, 16, QP), BF16),
            vmem((LAYERS, 4, 4, 8, 16, 128), BF16),
            vmem((64, DP), F32),
            vmem((LAYERS, 2, 4, 4, 16, DP), BF16),
            vmem((2, 256, 384), BF16),
            vmem((LAYERS, 256, 256), BF16),
            vmem((2, 4, 64, 128), BF16),
            vmem((LAYERS, 4, 64, 128), BF16),
            vmem((LAYERS, 4, 4, 16, DP), BF16),
            vmem((LAYERS, 2, 4, 16, DP), BF16),
            vmem((LAYERS, 2, 2, 16, DP), BF16),
            vmem((LAYERS, 2, 2, 16, DP), BF16),
            vmem((4, 16, D), BF16),
            vmem((D // 128, 384, 128), BF16),
            dma((16,)), dma((16,)), dma((8,)), dma((8,)),
            dma((LAYERS, 2, 8)), dma((LAYERS, 2, 8)), dma((LAYERS, 16, 2)), dma((LAYERS, 4)),
            dma((LAYERS, 2, 2, 4)), dma((LAYERS, 2, 2, 4)), dma((LAYERS, 2, 4)), dma((LAYERS, 2, 4)),
            dma((LAYERS,)), dma((LAYERS,)), dma((LAYERS, 11, 2)), dma((LAYERS, 11, 2)),
            dma((LAYERS,)), dma((LAYERS,)), dma((LAYERS,)), dma((LAYERS,)),
            dma((LAYERS, 6, 2)), dma((LAYERS, 6, 2)), dma((4,)), dma((4,)),
        ],
        compiler_params=pltpu.CompilerParams(
            collective_id=0, has_side_effects=True, vmem_limit_bytes=56 * 2**20
        ),
    )(latent[0].T, start_frame, norm_gains, both)
    return out.reshape(32, 2, D)


def solution(mesh):
    return jax.shard_map(
        local,
        mesh=mesh,
        in_specs=(
            P("tm", None, "head"),
            P("tm"),
            P(),
            P(None, "tm", None, "head"),
            P(None, "head", "tm"),
        ),
        out_specs=P("head", "tm", None),
        check_vma=False,
    )
```

```python
import jax
import jax.numpy as jnp
from jax import lax
from jax.experimental import pallas as pl
from jax.experimental.pallas import tpu as pltpu
from jax.sharding import PartitionSpec as P

NX, NY, NZ, ZLO = 4, 4, 16, 8
LAYERS = 2
D = 1920
DP = 2048
QP = 512
EPSILON = 1e-06
F32, BF16 = jnp.float32, jnp.bfloat16
MESH = pl.DeviceIdType.MESH


def dot(a, b):
    return jnp.dot(a, b, preferred_element_type=F32)


def dot_t(a, b):
    return lax.dot_general(a, b, (((1,), (1,)), ((), ())), preferred_element_type=F32)


def iota(shape, dim):
    return lax.broadcasted_iota(jnp.int32, shape, dim)


def onehot(mask):
    return jnp.where(mask, 1.0, 0.0).astype(BF16)


def kernel(
    lat_ref, start_ref, gain_ref, wloc_ref, out_ref,
    gains, latp, r1, y1, xq, wz, wf, wos, resid, xn, qkv, pkv, blb, bls, gs, rsb, rst, rso, fo, pick,
    az_s, az_r, ay_s, ay_r, wz_s, wz_r, wx_s, wx_r, wy_s, wy_r, wg_s, wg_r,
    wo_s, wo_r, ag_s, ag_r, kv_s, kv_r, bl_s, bl_r, rs_s, rs_r, fi_s, fi_r,
):
    tm, hd = lax.axis_index("tm"), lax.axis_index("head")
    y, x, zl = tm // 32, (tm // 8) % 4, tm % 8
    zh, c = hd // 2, hd % 2
    z = zh * 8 + zl

    def dev(xx, yy, zz, cc):
        return (yy * 32 + xx * 8 + zz % 8, (zz // 8) * 2 + cc)

    sends = []

    def send(src, dst, s_sem, r_sem, to):
        copy = pltpu.make_async_remote_copy(
            src_ref=src, dst_ref=dst, send_sem=s_sem, recv_sem=r_sem,
            device_id=to, device_id_type=MESH,
        )
        copy.start()
        sends.append(copy)

    def arrive(dst, sem):
        pltpu.make_async_copy(dst, dst, sem).wait()

    clip_x = z // 4
    pair = z % 4
    xu, xd, xo = (x + 1) % 4, (x + 3) % 4, (x + 2) % 4
    yu, yd, yo = (y + 1) % 4, (y + 3) % 4, (y + 2) % 4
    zu, zd = (z + 1) % 16, (z + 15) % 16

    barrier = pltpu.get_barrier_semaphore()

    def greet(to):
        pl.semaphore_signal(barrier, inc=1, device_id=to, device_id_type=MESH)

    for o in range(1, 16):
        greet(dev(x, y, (z + o) % 16, c))
    for o in range(4):
        for j in range(2):
            if o or j:
                greet(dev((x + o) % 4, y, z, (c + j) % 2))
    for o in range(1, 4):
        for j in range(2):
            greet(dev(x, (y + o) % 4, z, (c + j) % 2))
    for o in range(4):
        greet(dev((x + o) % 4, y, x * 4 + zl // 2, zh))

    wz[0, z] = wloc_ref[0]
    wz[1, z] = wloc_ref[1]
    pl.semaphore_wait(barrier, 15 + 7 + 6 + 4)

    reach = (8, 7)

    def chain_send(l, d, block, hop, k):
        to = dev(x, y, (z + hop) % 16 if d == 0 else (z + 16 - hop) % 16, c)
        send(wz.at[l, block], wz.at[l, block], wz_s.at[l, d, k - 1], wz_r.at[l, d, k - 1], to)

    def chain_start(l):
        for k in (1, 2):
            for d in range(2):
                chain_send(l, d, z, k, k)
        scatter_block(l, z, 0)

    def chain_step(l, i):
        for k in (2 * i - 1, 2 * i):
            for d in range(2):
                if k <= reach[d]:
                    block = (z + 16 - k) % 16 if d == 0 else (z + k) % 16
                    arrive(wz.at[l, block], wz_r.at[l, d, k - 1])
                    if k + 2 <= reach[d]:
                        chain_send(l, d, block, 2, k + 2)
                    scatter_block(l, block, k if d == 0 else 8 + k)

    def scatter_block(l, block, n):
        half, at = block // 8, block % 8
        t = half * 2 + c
        for b in range(2):
            j = (c + b) % 2
            src, dst = wz.at[l, block, j], wf.at[l, y, x, at]
            copy = pltpu.make_async_remote_copy(
                src_ref=src, dst_ref=dst, send_sem=wx_s.at[l, n, b], recv_sem=wx_r.at[l, x],
                device_id=dev(t, y, z, j), device_id_type=MESH,
            )
            if b == 0:
                own = pltpu.make_async_copy(src, dst, wx_r.at[l, x])

                @pl.when(t == x)
                def _():
                    own.start()

                @pl.when(t != x)
                def _():
                    copy.start()

                scattered.append((copy, t))
            else:
                copy.start()
                sends.append(copy)

    scattered = []

    def piece(l, yy, xx):
        return wf.at[l, yy, xx]

    def lanes(l, yy, xx, part):
        return wf.at[l, yy, xx, :, :, pl.ds(0, 384) if part == 0 else pl.ds(384, 128)]

    def ring_send(l, part):
        for p in range(4):
            if part == 0:
                arrive(piece(l, y, p), wx_r.at[l, p])
            block = lanes(l, y, p, part)
            for d, to in ((0, yu), (1, yd)):
                send(block, block, wy_s.at[l, part, d, p], wy_r.at[l, part, d, p], dev(x, to, z, c))

    def ring_forward(l, part, p):
        below, above = lanes(l, yd, p, part), lanes(l, yu, p, part)
        arrive(below, wy_r.at[l, part, 0, p])
        if p < 2:
            send(below, below, wg_s.at[l, part, p], wg_r.at[l, part, p], dev(x, yu, z, c))
        arrive(above, wy_r.at[l, part, 1, p])
        if p >= 2:
            send(above, above, wg_s.at[l, part, p], wg_r.at[l, part, p], dev(x, yd, z, c))

    def ring_end(l, part):
        for p in range(4):
            arrive(lanes(l, yo, p, part), wg_r.at[l, part, p])
        if part == 1:
            send(wf.at[l, :, :, :, :, pl.ds(384, 128)], wos.at[l], wo_s.at[l], wo_r.at[l], dev(x, y, z, 1 - c))

    chain_start(0)

    row, col = iota((256, 256), 0), iota((256, 256), 1)
    rows_by_z = onehot(col == ((row >> 2) & 3) * 64 + (row >> 4) * 4 + (row & 3))
    chan, pch = iota((480, QP), 0), iota((480, QP), 1)
    spread = onehot((chan == (pch >> 4) * 15 + (pch & 15)) & ((pch & 15) != 15))
    moved = dot_t(rows_by_z, lat_ref[...]).astype(BF16)
    pad_row = jnp.where((iota((1, QP), 1) & 15) == 15, start_ref[0].astype(F32), 0.0)
    moved = dot(moved, spread) + pad_row
    latp[...] = moved.astype(BF16).reshape(16, 16, QP)

    own_z = pltpu.make_async_copy(latp.at[z], r1.at[z], az_r.at[0])
    own_z.start()

    def latent_send(o):
        to = (z + o) % 16
        send(latp.at[to], r1.at[z], az_s.at[o], az_r.at[o], dev(x, y, to, c))

    order = ((8, 7, 9, 6), (10, 5, 11, 4), (12, 3, 13, 2), (14, 1, 15))
    for i in range(1, 5):
        for o in order[i - 1]:
            latent_send(o)
        chain_step(0, i)
    rest, split = gain_ref[...], []
    for _ in range(3):
        split.append(rest.astype(BF16))
        rest = rest - split[-1].astype(F32)
    split = jnp.concatenate(split, axis=0)
    for q in range(4):
        base = q * 480 // 128 * 128
        width = min(640, D - base)
        chan, pch = iota((width, QP), 0) + (base - q * 480), iota((width, QP), 1)
        chosen = onehot((chan == (pch >> 4) * 15 + (pch & 15)) & ((pch & 15) != 15))
        parts = dot(split[:, base:base + width], chosen)
        gains[:, q * QP:(q + 1) * QP] = parts[:2] + parts[2:4] + parts[4:]

    own_z.wait()
    for o in range(1, 16):
        arrive(r1.at[(z + 16 - o) % 16], az_r.at[o])
    rows_by_y = onehot(col == ((row >> 1) & 15) * 16 + (row >> 5) * 2 + (row & 1))
    y1[...] = dot(rows_by_y, r1[...].reshape(256, QP)).astype(BF16).reshape(8, 2, 16, QP)
    def latent_pass(o, par):
        to = (y + o) % 4
        return pltpu.make_async_remote_copy(
            src_ref=y1.at[to * 2 + par], dst_ref=xq.at[:, c, par, y % 2],
            send_sem=ay_s.at[o, par], recv_sem=ay_r.at[par, y % 2, c],
            device_id=dev(x, to, z, y // 2), device_id_type=MESH,
        )

    for par in (1, 0):
        for o in (1, 3, 2):
            copy = latent_pass(o, par)
            copy.start()
            sends.append(copy)

        @pl.when(c == y // 2)
        def _():
            pltpu.make_async_copy(y1.at[y * 2 + par], xq.at[:, c, par, y % 2], ay_r.at[par, y % 2, c]).start()

        @pl.when(c != y // 2)
        def _():
            latent_pass(0, par).start()

    chain_start(1)
    ring_send(0, 0)
    chain_step(1, 1)

    for par in range(2):
        for e in range(2):
            for j in range(2):
                arrive(xq.at[:, j, par, e], ay_r.at[par, e, j])
    for h in range(4):
        resid[:, h * QP:(h + 1) * QP] = xq[h // 2, h % 2].reshape(64, QP).astype(F32)

    real = (iota((1, DP), 1) & 15) != 15

    def slot(k, e):
        return slice((k * 2 + e) * 16, (k * 2 + e + 1) * 16)

    def norm_rows(l, k, e):
        rows = resid[slot(k, e)]
        square = jnp.where(real, rows * rows, 0.0)
        mean_square = jnp.sum(square, axis=1, keepdims=True) * (1.0 / D)
        normed = jnp.where(real, rows * lax.rsqrt(mean_square + EPSILON) * gains[l:l + 1], rows)
        xn[l, k, x, c * 2 + e] = normed.astype(BF16)

    def rows_of(l, k, xx, e):
        return xn.at[l, k, xx, c * 2 + e]

    def both_of(l, k, xx, cc):
        return xn.at[l, k, xx, pl.ds(cc * 2, 2)]

    def gather_copy(l, block, n, k, to):
        send(block, block, ag_s.at[l, n, k], ag_r.at[l, n, k], to)

    def gather_send(l, k):
        up, down = dev(xu, y, z, c), dev(xd, y, z, c)
        gather_copy(l, rows_of(l, k, x, 0), 0, k, up)
        gather_copy(l, rows_of(l, k, x, 1), 1, k, down)
        gather_copy(l, rows_of(l, k, x, 1), 2, k, up)
        gather_copy(l, rows_of(l, k, x, 0), 3, k, down)
        gather_copy(l, both_of(l, k, x, c), 4, k, dev(x, y, z, 1 - c))

    def gather_forward(l, k):
        arrive(rows_of(l, k, xd, 0), ag_r.at[l, 0, k])
        gather_copy(l, rows_of(l, k, xd, 0), 5, k, dev(xu, y, z, c))
        arrive(rows_of(l, k, xu, 1), ag_r.at[l, 1, k])
        gather_copy(l, rows_of(l, k, xu, 1), 6, k, dev(xd, y, z, c))

    def gather_sides(l, k):
        sibling = dev(x, y, z, 1 - c)
        arrive(rows_of(l, k, xd, 1), ag_r.at[l, 2, k])
        gather_copy(l, both_of(l, k, xd, c), 7, k, sibling)
        arrive(rows_of(l, k, xu, 0), ag_r.at[l, 3, k])
        gather_copy(l, both_of(l, k, xu, c), 8, k, sibling)

    def gather_far(l, k):
        arrive(rows_of(l, k, xo, 0), ag_r.at[l, 5, k])
        arrive(rows_of(l, k, xo, 1), ag_r.at[l, 6, k])
        gather_copy(l, both_of(l, k, xo, c), 9, k, dev(x, y, z, 1 - c))

    def gather_end(l, k):
        for xx, n in ((x, 4), (xd, 7), (xu, 8), (xo, 9)):
            arrive(both_of(l, k, xx, 1 - c), ag_r.at[l, n, k])

    def project(l, k):
        weight = wf[l, :, :, :, :, :384].reshape(DP, 384)
        qkv[k] = dot(xn[l, k].reshape(256, DP), weight).astype(BF16)

    lane = iota((1, 128), 1)
    frame = iota((1, 256), 1) & 1

    def first_frame(p):
        tile = xn[0, p, clip_x, y, :, :128].astype(F32)
        spot = (iota((16, 128), 0) == (pair * 2 + p) * 2) & (iota((16, 128), 1) == 15)
        kept = jnp.where(spot, tile, 0.0)
        return jnp.sum(jnp.sum(kept, axis=1, keepdims=True), axis=0, keepdims=True)

    def attend(p, prev_keys, prev_values, visible):
        queries = qkv[p, :, :128] * jnp.asarray(0.125, BF16)
        keys, values = qkv[p, :, 128:256], qkv[p, :, 256:384]
        parts = []
        for hh in range(2):
            mine = (lane // 64) == hh
            q = jnp.where(mine, queries, jnp.zeros_like(queries))
            own = dot_t(q, keys)
            past = jnp.where(visible, dot_t(q, prev_keys), -jnp.inf)
            highest = jnp.maximum(jnp.max(own, axis=1, keepdims=True), jnp.max(past, axis=1, keepdims=True))
            own, past = jnp.exp(own - highest), jnp.exp(past - highest)
            scale = 1.0 / (jnp.sum(own, axis=1, keepdims=True) + jnp.sum(past, axis=1, keepdims=True))
            parts.append(
                dot((own * scale).astype(BF16), values) + dot((past * scale).astype(BF16), prev_values)
            )
        return jnp.where(lane < 64, parts[0], parts[1]).astype(BF16)

    gather_like = pl.ds(128, 256)
    for k in (1, 0):
        norm_rows(0, k, 0)
        norm_rows(0, k, 1)
        gather_send(0, k)
    chain_step(1, 2)
    gather_forward(0, 1)
    ring_forward(0, 0, 0)
    gather_forward(0, 0)
    ring_forward(0, 0, 1)
    gather_sides(0, 1)
    gather_sides(0, 0)
    chain_step(1, 3)
    ring_forward(0, 0, 2)
    gather_far(0, 1)
    gather_far(0, 0)
    ring_forward(0, 0, 3)
    ring_send(0, 1)
    chain_step(1, 4)
    ring_end(0, 0)

    def drop_pads():
        for b in range(D // 128):
            first, width = window(b)
            a, ch = iota((width, 128), 0) + first, iota((width, 128), 1) + b * 128
            group = (ch * 4370) >> 16
            pick[b, :width] = onehot(a == group * 16 + (ch - group * 15))

    def window(b):
        first = ((b * 128 // 15) * 16 + (b * 128) % 15) // 128 * 128
        return first, min(384, DP - first)

    last = []

    def finish(k):
        refined = resid[k * 32:(k + 1) * 32].astype(BF16)
        for b in range(D // 128):
            first, width = window(b)
            packed = dot(refined[:, first:first + width], pick[b, :width]).astype(BF16)
            fo[k, :, :, b * 128:(b + 1) * 128] = packed.reshape(2, 16, 128)
        to_z = pair * 2 + k + 8 * c
        for e in range(2):
            copy = pltpu.make_async_remote_copy(
                src_ref=fo.at[k, e], dst_ref=out_ref.at[x], send_sem=fi_s.at[k, e], recv_sem=fi_r.at[x],
                device_id=dev(clip_x, y, to_z, e), device_id_type=MESH,
            )
            own = pltpu.make_async_copy(fo.at[k, e], out_ref.at[x], fi_r.at[x])
            here = (clip_x == x) & (to_z == z) & (c == e)
            last.append((copy, here))
            launch(copy, own, here)

    def launch(copy, own, here):
        @pl.when(here)
        def _():
            own.start()

        @pl.when(jnp.logical_not(here))
        def _():
            copy.start()

    for l in range(LAYERS):
        gather_end(l, 1)
        project(l, 1)
        send(qkv.at[1, :, gather_like], pkv.at[l], kv_s.at[l], kv_r.at[l], dev(x, y, zu, c))
        if l == 1:
            gather_sides(l, 0)
            gather_far(l, 0)
        gather_end(l, 0)
        project(l, 0)
        if l == 0:
            starts = [first_frame(p) for p in range(2)]

        def pass_blended(p):
            theirs = blb.at[p, :, pl.ds((1 - c) * 2, 2)]
            send(theirs, bls.at[l, p], bl_s.at[l, p], bl_r.at[l, p], dev(x, y, z, 1 - c))

        see = frame.astype(F32) >= starts[1]
        blb[1] = attend(1, qkv[0, :, 128:256], qkv[0, :, 256:384], see).reshape(4, 4, 16, 128)
        pass_blended(1)
        for p in range(4):
            ring_forward(l, 1, p)
        if l == 0:
            ring_send(1, 0)
            drop_pads()
        arrive(pkv.at[l], kv_r.at[l])
        see = (frame.astype(F32) >= starts[0]) & (pair > 0)
        blb[0] = attend(0, pkv[l, :, :128], pkv[l, :, 128:], see).reshape(4, 4, 16, 128)
        pass_blended(0)
        ring_end(l, 1)
        arrive(wos.at[l], wo_r.at[l])
        weight = jnp.concatenate([wf[l, :, :, :, :, 384:], wos[l]], axis=4).reshape(DP, 256)

        def update(k):
            arrive(bls.at[l, k], bl_r.at[l, k])
            mine = blb[k, :, pl.ds(c * 2, 2)].reshape(128, 128)
            blended = jnp.concatenate([mine, bls[l, k].reshape(128, 128)], axis=1)
            gs[l, k] = dot_t(blended, weight).astype(BF16).reshape(4, 2, 16, DP)

        up, down = dev(xu, y, z, c), dev(xd, y, z, c)

        def scatter_copy(src, dst, n, k, to):
            send(src, dst, rs_s.at[l, n, k], rs_r.at[l, n, k], to)

        def scatter_far(k):
            scatter_copy(gs.at[l, k, xo, 0], rst.at[l, 0, k], 0, k, up)
            scatter_copy(gs.at[l, k, xo, 1], rst.at[l, 1, k], 1, k, down)

        def scatter_plain(k):
            scatter_copy(gs.at[l, k, xu, 1], rsb.at[l, 0, k, 1], 2, k, up)
            scatter_copy(gs.at[l, k, xd, 0], rsb.at[l, 1, k, 0], 3, k, down)

        def scatter_sum(k):
            arrive(rst.at[l, 0, k], rs_r.at[l, 0, k])
            rso[l, 0, k] = (gs[l, k, xu, 0].astype(F32) + rst[l, 0, k].astype(F32)).astype(BF16)
            scatter_copy(rso.at[l, 0, k], rsb.at[l, 0, k, 0], 4, k, up)
            arrive(rst.at[l, 1, k], rs_r.at[l, 1, k])
            rso[l, 1, k] = (gs[l, k, xd, 1].astype(F32) + rst[l, 1, k].astype(F32)).astype(BF16)
            scatter_copy(rso.at[l, 1, k], rsb.at[l, 1, k, 1], 5, k, down)

        update(1)
        scatter_far(1)
        scatter_plain(1)
        update(0)
        scatter_far(0)
        scatter_sum(1)
        scatter_plain(0)
        scatter_sum(0)
        if l == 0:
            ring_forward(1, 0, 0)
            ring_forward(1, 0, 1)
        drain_upto = len(sends)
        for k in (1, 0):
            arrive(rsb.at[l, 0, k, 1], rs_r.at[l, 2, k])
            arrive(rsb.at[l, 1, k, 0], rs_r.at[l, 3, k])
            arrive(rsb.at[l, 0, k, 0], rs_r.at[l, 4, k])
            arrive(rsb.at[l, 1, k, 1], rs_r.at[l, 5, k])
            for e in range(2):
                total = gs[l, k, x, e].astype(F32) + rsb[l, 0, k, e].astype(F32) + rsb[l, 1, k, e].astype(F32)
                resid[slot(k, e)] += total
                if l == 0:
                    norm_rows(1, k, e)
            if l == 0:
                gather_send(1, k)
            else:
                finish(k)
        if l == 0:
            gather_forward(1, 1)
            ring_forward(1, 0, 2)
            ring_forward(1, 0, 3)
            gather_forward(1, 0)
            gather_sides(1, 1)
            ring_send(1, 1)
            for copy in sends[:drain_upto]:
                copy.wait_send()
            del sends[:drain_upto]
            gather_far(1, 1)
            ring_end(1, 0)

    for p in range(4):
        arrive(out_ref.at[p], fi_r.at[p])

    def settle(copy, there):
        @pl.when(there)
        def _():
            copy.wait_send()

    for copy, here in last:
        settle(copy, jnp.logical_not(here))
    for par in range(2):
        settle(latent_pass(0, par), c != y // 2)
    for copy, t in scattered:
        settle(copy, t != x)
    for copy in sends:
        copy.wait_send()


def local(latent, start_frame, norm_gains, qkv_weight, out_weight):
    both = jnp.concatenate([qkv_weight, out_weight.transpose(0, 2, 1)[:, :, None, :]], axis=2)
    both = both.reshape(LAYERS, 15, 4, 2, 128).transpose(0, 3, 1, 2, 4).reshape(LAYERS, 2, 15, QP)
    both = jnp.pad(both, ((0, 0), (0, 0), (0, 1), (0, 0)))
    dma = pltpu.SemaphoreType.DMA
    vmem = pltpu.VMEM
    out = pl.pallas_call(
        kernel,
        out_shape=jax.ShapeDtypeStruct((4, 16, D), BF16),
        in_specs=[
            pl.BlockSpec(memory_space=vmem),
            pl.BlockSpec(memory_space=pltpu.SMEM),
            pl.BlockSpec(memory_space=vmem),
            pl.BlockSpec(memory_space=vmem),
        ],
        out_specs=pl.BlockSpec(memory_space=vmem),
        scratch_shapes=[
            vmem((LAYERS, DP), F32),
            vmem((16, 16, QP), BF16),
            vmem((16, 16, QP), BF16),
            vmem((8, 2, 16, QP), BF16),
            vmem((2, 2, 2, 2, 16, QP), BF16),
            vmem((LAYERS, 16, 2, 16, QP), BF16),
            vmem((LAYERS, 4, 4, 8, 16, QP), BF16),
            vmem((LAYERS, 4, 4, 8, 16, 128), BF16),
            vmem((64, DP), F32),
            vmem((LAYERS, 2, 4, 4, 16, DP), BF16),
            vmem((2, 256, 384), BF16),
            vmem((LAYERS, 256, 256), BF16),
            vmem((2, 4, 4, 16, 128), BF16),
            vmem((LAYERS, 2, 4, 2, 16, 128), BF16),
            vmem((LAYERS, 2, 4, 2, 16, DP), BF16),
            vmem((LAYERS, 2, 2, 2, 16, DP), BF16),
            vmem((LAYERS, 2, 2, 16, DP), BF16),
            vmem((LAYERS, 2, 2, 16, DP), BF16),
            vmem((2, 2, 16, D), BF16),
            vmem((D // 128, 384, 128), BF16),
            dma((16,)), dma((16,)), dma((4, 2)), dma((2, 2, 2)),
            dma((LAYERS, 2, 8)), dma((LAYERS, 2, 8)), dma((LAYERS, 16, 2)), dma((LAYERS, 4)),
            dma((LAYERS, 2, 2, 4)), dma((LAYERS, 2, 2, 4)), dma((LAYERS, 2, 4)), dma((LAYERS, 2, 4)),
            dma((LAYERS,)), dma((LAYERS,)), dma((LAYERS, 10, 2)), dma((LAYERS, 10, 2)),
            dma((LAYERS,)), dma((LAYERS,)), dma((LAYERS, 2)), dma((LAYERS, 2)),
            dma((LAYERS, 6, 2)), dma((LAYERS, 6, 2)), dma((2, 2)), dma((4,)),
        ],
        compiler_params=pltpu.CompilerParams(
            collective_id=0, has_side_effects=True, vmem_limit_bytes=56 * 2**20
        ),
    )(latent[0].T, start_frame, norm_gains, both)
    return out.reshape(32, 2, D)


def solution(mesh):
    return jax.shard_map(
        local,
        mesh=mesh,
        in_specs=(
            P("tm", None, "head"),
            P("tm"),
            P(),
            P(None, "tm", None, "head"),
            P(None, "head", "tm"),
        ),
        out_specs=P("head", "tm", None),
        check_vma=False,
    )
```

```python
import jax
import jax.numpy as jnp
from jax import lax
from jax.experimental import pallas as pl
from jax.experimental.pallas import tpu as pltpu
from jax.sharding import PartitionSpec as P

NX, NY, NZ, ZLO = 4, 4, 16, 8
LAYERS = 2
D = 1920
DP = 2048
QP = 512
EPSILON = 1e-06
F32, BF16 = jnp.float32, jnp.bfloat16
MESH = pl.DeviceIdType.MESH


def dot(a, b):
    return jnp.dot(a, b, preferred_element_type=F32)


def dot_t(a, b):
    return lax.dot_general(a, b, (((1,), (1,)), ((), ())), preferred_element_type=F32)


def iota(shape, dim):
    return lax.broadcasted_iota(jnp.int32, shape, dim)


def onehot(mask):
    return jnp.where(mask, 1.0, 0.0).astype(BF16)


def kernel(
    lat_ref, start_ref, gain_ref, wloc_ref, out_ref,
    gains, latp, r1, y1, xq, wz, wf, wos, resid, xn, qkv, pkv, blb, bls, gs, rsb, rst, rso, fo, pick,
    az_s, az_r, ay_s, ay_r, wz_s, wz_r, wx_s, wx_r, wy_s, wy_r, wg_s, wg_r,
    wo_s, wo_r, ag_s, ag_r, kv_s, kv_r, bl_s, bl_r, rs_s, rs_r, fi_s, fi_r,
):
    tm, hd = lax.axis_index("tm"), lax.axis_index("head")
    y, x, zl = tm // 32, (tm // 8) % 4, tm % 8
    zh, c = hd // 2, hd % 2
    z = zh * 8 + zl

    def dev(xx, yy, zz, cc):
        return (yy * 32 + xx * 8 + zz % 8, (zz // 8) * 2 + cc)

    sends = []

    def send(src, dst, s_sem, r_sem, to):
        copy = pltpu.make_async_remote_copy(
            src_ref=src, dst_ref=dst, send_sem=s_sem, recv_sem=r_sem,
            device_id=to, device_id_type=MESH,
        )
        copy.start()
        sends.append(copy)

    def arrive(dst, sem):
        pltpu.make_async_copy(dst, dst, sem).wait()

    clip_x = z // 4
    pair = z % 4
    xu, xd, xo = (x + 1) % 4, (x + 3) % 4, (x + 2) % 4
    yu, yd, yo = (y + 1) % 4, (y + 3) % 4, (y + 2) % 4
    zu, zd = (z + 1) % 16, (z + 15) % 16

    barrier = pltpu.get_barrier_semaphore()

    def greet(to):
        pl.semaphore_signal(barrier, inc=1, device_id=to, device_id_type=MESH)

    for o in range(1, 16):
        greet(dev(x, y, (z + o) % 16, c))
    for o in range(4):
        for j in range(2):
            if o or j:
                greet(dev((x + o) % 4, y, z, (c + j) % 2))
    for o in range(1, 4):
        for j in range(2):
            greet(dev(x, (y + o) % 4, z, (c + j) % 2))
    for o in range(4):
        greet(dev((x + o) % 4, y, x * 4 + zl // 2, zh))

    wz[0, z] = wloc_ref[0]
    wz[1, z] = wloc_ref[1]
    pl.semaphore_wait(barrier, 15 + 7 + 6 + 4)

    reach = (8, 7)

    def chain_send(l, d, block, hop, k):
        to = dev(x, y, (z + hop) % 16 if d == 0 else (z + 16 - hop) % 16, c)
        send(wz.at[l, block], wz.at[l, block], wz_s.at[l, d, k - 1], wz_r.at[l, d, k - 1], to)

    def chain_start(l):
        for k in (1, 2):
            for d in range(2):
                chain_send(l, d, z, k, k)
        scatter_block(l, z, 0)

    def chain_step(l, i):
        for k in (2 * i - 1, 2 * i):
            for d in range(2):
                if k <= reach[d]:
                    block = (z + 16 - k) % 16 if d == 0 else (z + k) % 16
                    arrive(wz.at[l, block], wz_r.at[l, d, k - 1])
                    if k + 2 <= reach[d]:
                        chain_send(l, d, block, 2, k + 2)
                    scatter_block(l, block, k if d == 0 else 8 + k)

    def scatter_block(l, block, n):
        half, at = block // 8, block % 8
        t = half * 2 + c
        for b in range(2):
            j = (c + b) % 2
            src, dst = wz.at[l, block, j], wf.at[l, y, x, at]
            copy = pltpu.make_async_remote_copy(
                src_ref=src, dst_ref=dst, send_sem=wx_s.at[l, n, b], recv_sem=wx_r.at[l, x],
                device_id=dev(t, y, z, j), device_id_type=MESH,
            )
            if b == 0:
                own = pltpu.make_async_copy(src, dst, wx_r.at[l, x])

                @pl.when(t == x)
                def _():
                    own.start()

                @pl.when(t != x)
                def _():
                    copy.start()

                scattered.append((copy, t))
            else:
                copy.start()
                sends.append(copy)

    scattered = []

    def piece(l, yy, xx):
        return wf.at[l, yy, xx]

    def lanes(l, yy, xx, part):
        return wf.at[l, yy, xx, :, :, pl.ds(0, 384) if part == 0 else pl.ds(384, 128)]

    def ring_send(l, part):
        for n in range(4):
            if part == 0 and n < 2:
                for p in (n, n + 2):
                    arrive(piece(l, y, p), wx_r.at[l, p])
            for d, to, p in ((0, yu, n), (1, yd, (n + 2) % 4)):
                block = lanes(l, y, p, part)
                send(block, block, wy_s.at[l, part, d, p], wy_r.at[l, part, d, p], dev(x, to, z, c))

    def ring_forward(l, part, n):
        for d, yy, to, p in ((0, yd, yu, n), (1, yu, yd, (n + 2) % 4)):
            block = lanes(l, yy, p, part)
            arrive(block, wy_r.at[l, part, d, p])
            if n < 2:
                send(block, block, wg_s.at[l, part, p], wg_r.at[l, part, p], dev(x, to, z, c))

    def ring_end(l, part):
        for p in range(4):
            arrive(lanes(l, yo, p, part), wg_r.at[l, part, p])
        if part == 1:
            send(wf.at[l, :, :, :, :, pl.ds(384, 128)], wos.at[l], wo_s.at[l], wo_r.at[l], dev(x, y, z, 1 - c))

    chain_start(0)

    row, col = iota((256, 256), 0), iota((256, 256), 1)
    rows_by_z = onehot(col == ((row >> 2) & 3) * 64 + (row >> 4) * 4 + (row & 3))
    chan, pch = iota((480, QP), 0), iota((480, QP), 1)
    spread = onehot((chan == (pch >> 4) * 15 + (pch & 15)) & ((pch & 15) != 15))
    moved = dot_t(rows_by_z, lat_ref[...]).astype(BF16)
    pad_row = jnp.where((iota((1, QP), 1) & 15) == 15, start_ref[0].astype(F32), 0.0)
    moved = dot(moved, spread) + pad_row
    latp[...] = moved.astype(BF16).reshape(16, 16, QP)

    own_z = pltpu.make_async_copy(latp.at[z], r1.at[z], az_r.at[0])
    own_z.start()

    def latent_send(o):
        to = (z + o) % 16
        send(latp.at[to], r1.at[z], az_s.at[o], az_r.at[o], dev(x, y, to, c))

    order = ((8, 7, 9, 6), (10, 5, 11, 4), (12, 3, 13, 2), (14, 1, 15))
    for i in range(1, 5):
        for o in order[i - 1]:
            latent_send(o)
        chain_step(0, i)
    rest, split = gain_ref[...], []
    for _ in range(3):
        split.append(rest.astype(BF16))
        rest = rest - split[-1].astype(F32)
    split = jnp.concatenate(split, axis=0)
    for q in range(4):
        base = q * 480 // 128 * 128
        width = min(640, D - base)
        chan, pch = iota((width, QP), 0) + (base - q * 480), iota((width, QP), 1)
        chosen = onehot((chan == (pch >> 4) * 15 + (pch & 15)) & ((pch & 15) != 15))
        parts = dot(split[:, base:base + width], chosen)
        gains[:, q * QP:(q + 1) * QP] = parts[:2] + parts[2:4] + parts[4:]

    own_z.wait()
    for o in range(1, 16):
        arrive(r1.at[(z + 16 - o) % 16], az_r.at[o])
    rows_by_y = onehot(col == ((row >> 1) & 15) * 16 + (row >> 5) * 2 + (row & 1))
    y1[...] = dot(rows_by_y, r1[...].reshape(256, QP)).astype(BF16).reshape(8, 2, 16, QP)
    def latent_pass(o, par):
        to = (y + o) % 4
        return pltpu.make_async_remote_copy(
            src_ref=y1.at[to * 2 + par], dst_ref=xq.at[:, c, par, y % 2],
            send_sem=ay_s.at[o, par], recv_sem=ay_r.at[par, y % 2, c],
            device_id=dev(x, to, z, y // 2), device_id_type=MESH,
        )

    for par in (1, 0):
        for o in (1, 3, 2):
            copy = latent_pass(o, par)
            copy.start()
            sends.append(copy)

        @pl.when(c == y // 2)
        def _():
            pltpu.make_async_copy(y1.at[y * 2 + par], xq.at[:, c, par, y % 2], ay_r.at[par, y % 2, c]).start()

        @pl.when(c != y // 2)
        def _():
            latent_pass(0, par).start()

    chain_start(1)
    ring_send(0, 0)
    chain_step(1, 1)

    for par in range(2):
        for e in range(2):
            for j in range(2):
                arrive(xq.at[:, j, par, e], ay_r.at[par, e, j])
    for h in range(4):
        resid[:, h * QP:(h + 1) * QP] = xq[h // 2, h % 2].reshape(64, QP).astype(F32)

    real = (iota((1, DP), 1) & 15) != 15

    def slot(k, e):
        return slice((k * 2 + e) * 16, (k * 2 + e + 1) * 16)

    def norm_rows(l, k, e):
        rows = resid[slot(k, e)]
        square = jnp.where(real, rows * rows, 0.0)
        mean_square = jnp.sum(square, axis=1, keepdims=True) * (1.0 / D)
        normed = jnp.where(real, rows * lax.rsqrt(mean_square + EPSILON) * gains[l:l + 1], rows)
        xn[l, k, x, c * 2 + e] = normed.astype(BF16)

    def rows_of(l, k, xx, e):
        return xn.at[l, k, xx, c * 2 + e]

    def both_of(l, k, xx, cc):
        return xn.at[l, k, xx, pl.ds(cc * 2, 2)]

    def gather_copy(l, block, n, k, to):
        send(block, block, ag_s.at[l, n, k], ag_r.at[l, n, k], to)

    def gather_send(l, k):
        up, down = dev(xu, y, z, c), dev(xd, y, z, c)
        gather_copy(l, rows_of(l, k, x, 0), 0, k, up)
        gather_copy(l, rows_of(l, k, x, 1), 1, k, down)
        gather_copy(l, rows_of(l, k, x, 1), 2, k, up)
        gather_copy(l, rows_of(l, k, x, 0), 3, k, down)
        gather_copy(l, both_of(l, k, x, c), 4, k, dev(x, y, z, 1 - c))

    def gather_forward(l, k):
        arrive(rows_of(l, k, xd, 0), ag_r.at[l, 0, k])
        gather_copy(l, rows_of(l, k, xd, 0), 5, k, dev(xu, y, z, c))
        arrive(rows_of(l, k, xu, 1), ag_r.at[l, 1, k])
        gather_copy(l, rows_of(l, k, xu, 1), 6, k, dev(xd, y, z, c))

    def gather_sides(l, k):
        sibling = dev(x, y, z, 1 - c)
        arrive(rows_of(l, k, xd, 1), ag_r.at[l, 2, k])
        gather_copy(l, both_of(l, k, xd, c), 7, k, sibling)
        arrive(rows_of(l, k, xu, 0), ag_r.at[l, 3, k])
        gather_copy(l, both_of(l, k, xu, c), 8, k, sibling)

    def gather_far(l, k):
        arrive(rows_of(l, k, xo, 0), ag_r.at[l, 5, k])
        arrive(rows_of(l, k, xo, 1), ag_r.at[l, 6, k])
        gather_copy(l, both_of(l, k, xo, c), 9, k, dev(x, y, z, 1 - c))

    def gather_end(l, k):
        for xx, n in ((x, 4), (xd, 7), (xu, 8), (xo, 9)):
            arrive(both_of(l, k, xx, 1 - c), ag_r.at[l, n, k])

    def project(l, k):
        weight = wf[l, :, :, :, :, :384].reshape(DP, 384)
        qkv[k] = dot(xn[l, k].reshape(256, DP), weight).astype(BF16)

    lane = iota((1, 128), 1)
    frame = iota((1, 256), 1) & 1

    def first_frame(p):
        tile = xn[0, p, clip_x, y, :, :128].astype(F32)
        spot = (iota((16, 128), 0) == (pair * 2 + p) * 2) & (iota((16, 128), 1) == 15)
        kept = jnp.where(spot, tile, 0.0)
        return jnp.sum(jnp.sum(kept, axis=1, keepdims=True), axis=0, keepdims=True)

    def attend(p, prev_keys, prev_values, visible):
        queries = qkv[p, :, :128] * jnp.asarray(0.125, BF16)
        keys, values = qkv[p, :, 128:256], qkv[p, :, 256:384]
        parts = []
        for hh in range(2):
            mine = (lane // 64) == hh
            q = jnp.where(mine, queries, jnp.zeros_like(queries))
            own = dot_t(q, keys)
            past = jnp.where(visible, dot_t(q, prev_keys), -jnp.inf)
            highest = jnp.maximum(jnp.max(own, axis=1, keepdims=True), jnp.max(past, axis=1, keepdims=True))
            own, past = jnp.exp(own - highest), jnp.exp(past - highest)
            scale = 1.0 / (jnp.sum(own, axis=1, keepdims=True) + jnp.sum(past, axis=1, keepdims=True))
            parts.append(
                dot((own * scale).astype(BF16), values) + dot((past * scale).astype(BF16), prev_values)
            )
        return jnp.where(lane < 64, parts[0], parts[1]).astype(BF16)

    gather_like = pl.ds(128, 256)
    for k in (1, 0):
        norm_rows(0, k, 0)
        norm_rows(0, k, 1)
        gather_send(0, k)
    chain_step(1, 2)
    gather_forward(0, 1)
    ring_forward(0, 0, 0)
    gather_forward(0, 0)
    ring_forward(0, 0, 1)
    gather_sides(0, 1)
    gather_sides(0, 0)
    chain_step(1, 3)
    ring_forward(0, 0, 2)
    gather_far(0, 1)
    gather_far(0, 0)
    ring_forward(0, 0, 3)
    ring_send(0, 1)
    chain_step(1, 4)
    ring_end(0, 0)

    def drop_pads():
        for b in range(D // 128):
            first, width = window(b)
            a, ch = iota((width, 128), 0) + first, iota((width, 128), 1) + b * 128
            group = (ch * 4370) >> 16
            pick[b, :width] = onehot(a == group * 16 + (ch - group * 15))

    def window(b):
        first = ((b * 128 // 15) * 16 + (b * 128) % 15) // 128 * 128
        return first, min(384, DP - first)

    last = []

    def finish(k):
        refined = resid[k * 32:(k + 1) * 32].astype(BF16)
        for b in range(D // 128):
            first, width = window(b)
            packed = dot(refined[:, first:first + width], pick[b, :width]).astype(BF16)
            fo[k, :, :, b * 128:(b + 1) * 128] = packed.reshape(2, 16, 128)
        to_z = pair * 2 + k + 8 * c
        for e in range(2):
            copy = pltpu.make_async_remote_copy(
                src_ref=fo.at[k, e], dst_ref=out_ref.at[x], send_sem=fi_s.at[k, e], recv_sem=fi_r.at[x],
                device_id=dev(clip_x, y, to_z, e), device_id_type=MESH,
            )
            own = pltpu.make_async_copy(fo.at[k, e], out_ref.at[x], fi_r.at[x])
            here = (clip_x == x) & (to_z == z) & (c == e)
            last.append((copy, here))
            launch(copy, own, here)

    def launch(copy, own, here):
        @pl.when(here)
        def _():
            own.start()

        @pl.when(jnp.logical_not(here))
        def _():
            copy.start()

    for l in range(LAYERS):
        gather_end(l, 1)
        project(l, 1)
        send(qkv.at[1, :, gather_like], pkv.at[l], kv_s.at[l], kv_r.at[l], dev(x, y, zu, c))
        if l == 1:
            gather_sides(l, 0)
            gather_far(l, 0)
        gather_end(l, 0)
        project(l, 0)
        if l == 0:
            starts = [first_frame(p) for p in range(2)]

        def pass_blended(p):
            theirs = blb.at[p, :, pl.ds((1 - c) * 2, 2)]
            send(theirs, bls.at[l, p], bl_s.at[l, p], bl_r.at[l, p], dev(x, y, z, 1 - c))

        see = frame.astype(F32) >= starts[1]
        blb[1] = attend(1, qkv[0, :, 128:256], qkv[0, :, 256:384], see).reshape(4, 4, 16, 128)
        pass_blended(1)
        for p in range(4):
            ring_forward(l, 1, p)
        if l == 0:
            ring_send(1, 0)
            drop_pads()
        arrive(pkv.at[l], kv_r.at[l])
        see = (frame.astype(F32) >= starts[0]) & (pair > 0)
        blb[0] = attend(0, pkv[l, :, :128], pkv[l, :, 128:], see).reshape(4, 4, 16, 128)
        pass_blended(0)
        ring_end(l, 1)
        arrive(wos.at[l], wo_r.at[l])
        weight = jnp.concatenate([wf[l, :, :, :, :, 384:], wos[l]], axis=4).reshape(DP, 256)

        def update(k):
            arrive(bls.at[l, k], bl_r.at[l, k])
            mine = blb[k, :, pl.ds(c * 2, 2)].reshape(128, 128)
            blended = jnp.concatenate([mine, bls[l, k].reshape(128, 128)], axis=1)
            gs[l, k] = dot_t(blended, weight).astype(BF16).reshape(4, 2, 16, DP)

        up, down = dev(xu, y, z, c), dev(xd, y, z, c)

        def scatter_copy(src, dst, n, k, to):
            send(src, dst, rs_s.at[l, n, k], rs_r.at[l, n, k], to)

        def scatter_far(k):
            scatter_copy(gs.at[l, k, xo, 0], rst.at[l, 0, k], 0, k, up)
            scatter_copy(gs.at[l, k, xo, 1], rst.at[l, 1, k], 1, k, down)

        def scatter_plain(k):
            scatter_copy(gs.at[l, k, xu, 1], rsb.at[l, 0, k, 1], 2, k, up)
            scatter_copy(gs.at[l, k, xd, 0], rsb.at[l, 1, k, 0], 3, k, down)

        def scatter_sum(k):
            arrive(rst.at[l, 0, k], rs_r.at[l, 0, k])
            rso[l, 0, k] = (gs[l, k, xu, 0].astype(F32) + rst[l, 0, k].astype(F32)).astype(BF16)
            scatter_copy(rso.at[l, 0, k], rsb.at[l, 0, k, 0], 4, k, up)
            arrive(rst.at[l, 1, k], rs_r.at[l, 1, k])
            rso[l, 1, k] = (gs[l, k, xd, 1].astype(F32) + rst[l, 1, k].astype(F32)).astype(BF16)
            scatter_copy(rso.at[l, 1, k], rsb.at[l, 1, k, 1], 5, k, down)

        update(1)
        scatter_far(1)
        scatter_plain(1)
        update(0)
        scatter_far(0)
        scatter_sum(1)
        scatter_plain(0)
        scatter_sum(0)
        if l == 0:
            ring_forward(1, 0, 0)
            ring_forward(1, 0, 1)
        drain_upto = len(sends)
        for k in (1, 0):
            arrive(rsb.at[l, 0, k, 1], rs_r.at[l, 2, k])
            arrive(rsb.at[l, 1, k, 0], rs_r.at[l, 3, k])
            arrive(rsb.at[l, 0, k, 0], rs_r.at[l, 4, k])
            arrive(rsb.at[l, 1, k, 1], rs_r.at[l, 5, k])
            for e in range(2):
                total = gs[l, k, x, e].astype(F32) + rsb[l, 0, k, e].astype(F32) + rsb[l, 1, k, e].astype(F32)
                resid[slot(k, e)] += total
                if l == 0:
                    norm_rows(1, k, e)
            if l == 0:
                gather_send(1, k)
            else:
                finish(k)
        if l == 0:
            gather_forward(1, 1)
            ring_forward(1, 0, 2)
            ring_forward(1, 0, 3)
            gather_forward(1, 0)
            gather_sides(1, 1)
            ring_send(1, 1)
            for copy in sends[:drain_upto]:
                copy.wait_send()
            del sends[:drain_upto]
            gather_far(1, 1)
            ring_end(1, 0)

    for p in range(4):
        arrive(out_ref.at[p], fi_r.at[p])

    def settle(copy, there):
        @pl.when(there)
        def _():
            copy.wait_send()

    for copy, here in last:
        settle(copy, jnp.logical_not(here))
    for par in range(2):
        settle(latent_pass(0, par), c != y // 2)
    for copy, t in scattered:
        settle(copy, t != x)
    for copy in sends:
        copy.wait_send()


def local(latent, start_frame, norm_gains, qkv_weight, out_weight):
    both = jnp.concatenate([qkv_weight, out_weight.transpose(0, 2, 1)[:, :, None, :]], axis=2)
    both = both.reshape(LAYERS, 15, 4, 2, 128).transpose(0, 3, 1, 2, 4).reshape(LAYERS, 2, 15, QP)
    both = jnp.pad(both, ((0, 0), (0, 0), (0, 1), (0, 0)))
    dma = pltpu.SemaphoreType.DMA
    vmem = pltpu.VMEM
    out = pl.pallas_call(
        kernel,
        out_shape=jax.ShapeDtypeStruct((4, 16, D), BF16),
        in_specs=[
            pl.BlockSpec(memory_space=vmem),
            pl.BlockSpec(memory_space=pltpu.SMEM),
            pl.BlockSpec(memory_space=vmem),
            pl.BlockSpec(memory_space=vmem),
        ],
        out_specs=pl.BlockSpec(memory_space=vmem),
        scratch_shapes=[
            vmem((LAYERS, DP), F32),
            vmem((16, 16, QP), BF16),
            vmem((16, 16, QP), BF16),
            vmem((8, 2, 16, QP), BF16),
            vmem((2, 2, 2, 2, 16, QP), BF16),
            vmem((LAYERS, 16, 2, 16, QP), BF16),
            vmem((LAYERS, 4, 4, 8, 16, QP), BF16),
            vmem((LAYERS, 4, 4, 8, 16, 128), BF16),
            vmem((64, DP), F32),
            vmem((LAYERS, 2, 4, 4, 16, DP), BF16),
            vmem((2, 256, 384), BF16),
            vmem((LAYERS, 256, 256), BF16),
            vmem((2, 4, 4, 16, 128), BF16),
            vmem((LAYERS, 2, 4, 2, 16, 128), BF16),
            vmem((LAYERS, 2, 4, 2, 16, DP), BF16),
            vmem((LAYERS, 2, 2, 2, 16, DP), BF16),
            vmem((LAYERS, 2, 2, 16, DP), BF16),
            vmem((LAYERS, 2, 2, 16, DP), BF16),
            vmem((2, 2, 16, D), BF16),
            vmem((D // 128, 384, 128), BF16),
            dma((16,)), dma((16,)), dma((4, 2)), dma((2, 2, 2)),
            dma((LAYERS, 2, 8)), dma((LAYERS, 2, 8)), dma((LAYERS, 16, 2)), dma((LAYERS, 4)),
            dma((LAYERS, 2, 2, 4)), dma((LAYERS, 2, 2, 4)), dma((LAYERS, 2, 4)), dma((LAYERS, 2, 4)),
            dma((LAYERS,)), dma((LAYERS,)), dma((LAYERS, 10, 2)), dma((LAYERS, 10, 2)),
            dma((LAYERS,)), dma((LAYERS,)), dma((LAYERS, 2)), dma((LAYERS, 2)),
            dma((LAYERS, 6, 2)), dma((LAYERS, 6, 2)), dma((2, 2)), dma((4,)),
        ],
        compiler_params=pltpu.CompilerParams(
            collective_id=0, has_side_effects=True, vmem_limit_bytes=56 * 2**20
        ),
    )(latent[0].T, start_frame, norm_gains, both)
    return out.reshape(32, 2, D)


def solution(mesh):
    return jax.shard_map(
        local,
        mesh=mesh,
        in_specs=(
            P("tm", None, "head"),
            P("tm"),
            P(),
            P(None, "tm", None, "head"),
            P(None, "head", "tm"),
        ),
        out_specs=P("head", "tm", None),
        check_vma=False,
    )
```
